128 devices in a mesh: dp: 4 (over z_lo, core), ctx: 32 (over x, y, z_hi).
Axes of the slice: x: 4, y: 4, z: 4 (z_hi: 2, z_lo: 2; z = z_hi * 2 + z_lo), core: 2. Of those that a mesh axis runs over, the one named last changes fastest.
Arguments:
- hidden_x: bfloat16 [4, 16384, 2048], P('dp', 'ctx'), may hold values from -6 to 6
- b_proj: bfloat16 [4, 16384, 256], P('dp', 'ctx'), may hold values from -0.5 to 0.5
- c_proj: bfloat16 [4, 16384, 256], P('dp', 'ctx'), may hold values from -0.5 to 0.5
- dt_raw: float32 [4, 16384, 64], P('dp', 'ctx'), may hold values from -3 to 3
- span_start: int32 [4, 16384], P('dp', 'ctx'), may hold values 0 or 1
- a_log: float32 [64], replicated, may hold values from -9 to -3.4
- skip_gain: float32 [64], replicated, may hold values from 0.5 to 1.5
- dt_bias: float32 [64], replicated, may hold values from -0.5 to 0.5
- out_grad: bfloat16 [4, 16384, 2048], P('dp', 'ctx'), may hold values from -6 to 6
Outputs:
- mixed: bfloat16 [4, 16384, 2048], P('dp', 'ctx')
- grad_x: bfloat16 [4, 16384, 2048], P('dp', 'ctx')
- grad_b: bfloat16 [4, 16384, 256], P('dp', 'ctx')
- grad_c: bfloat16 [4, 16384, 256], P('dp', 'ctx')
- grad_dt: float32 [4, 16384, 64], P('dp', 'ctx')
- grad_a_log: float32 [64], replicated
- grad_skip: float32 [64], replicated
- grad_dt_bias: float32 [64], replicated
The draws below stay inside these ranges and needn't reach their ends.
All inputs are finite; a program needn't handle non-finite values. No bound on the sum of `span_start` on one device may be relied on, other than what follows from the above.
Results may differ from the reference program's by a relative error of at most 0.0095.
Values sent between devices are 32-bit elements; how exact they have to be, the bound alone decides.
A program may use at most 320 MiB of HBM per device.

```python
import jax
import jax.numpy as jnp
from jax import lax

H = 64
P_SIZE = 32
N = 64
G = 4
STRETCH = 256
SEQ = 16384
ROLLS = 4
N_DP = 4
N_CTX = 32


def plant(result, stream_key, least, largest):
    index_at = [jax.random.randint(jax.random.fold_in(stream_key, axis), (), 0, length) for axis, length in enumerate(result.shape)]
    widest = result.shape.index(max(result.shape))
    beside = index_at[:widest] + [(index_at[widest] + 1) % result.shape[widest]] + index_at[widest + 1:]
    return result.at[tuple(index_at)].set(least).at[tuple(beside)].set(largest)


def levels(stream_key, extent, cuts, least, top_value):
    loudness = 1.0
    for axis_at, blocks in cuts:
        steps = jax.random.uniform(jax.random.fold_in(jax.random.fold_in(stream_key, 6), axis_at), (blocks,), jnp.float32, least / len(cuts), top_value / len(cuts))
        loudness = loudness * jnp.repeat(jnp.exp(steps), extent[axis_at] // blocks).reshape((-1,) + (1,) * (len(extent) - 1 - axis_at))
    return loudness


def bell_draw(rng, shape, deviation, reach, cuts=(), kind=jnp.bfloat16):
    entries = deviation * jax.random.normal(rng, shape, jnp.float32)
    if cuts:
        entries = entries * levels(rng, shape, cuts, -0.22, 0.18)
    return jnp.clip(entries, -reach, reach).astype(kind)


def setup_inputs(seed: int = 0) -> dict:
    seeds = jax.random.split(jax.random.key(seed), 10)
    return {
        "hidden_x": bell_draw(seeds[0], (ROLLS, SEQ, H * P_SIZE), 1.0, 6.0, ((0, 4), (1, 32))),
        "b_proj": bell_draw(seeds[1], (ROLLS, SEQ, G * N), 0.08, 0.5, ((0, 4), (1, 32))),
        "c_proj": bell_draw(seeds[2], (ROLLS, SEQ, G * N), 0.08, 0.5, ((0, 4), (1, 32))),
        "dt_raw": bell_draw(seeds[3], (ROLLS, SEQ, H), 0.5, 3.0, ((0, 4), (1, 32)), jnp.float32),
        "span_start": plant((jax.random.randint(seeds[4], (ROLLS, SEQ), 0, 1024) < 1).astype(jnp.int32), jax.random.fold_in(seeds[4], 1), 0, 1),
        "a_log": jnp.clip(jax.random.uniform(seeds[5], (H,), jnp.float32, -9.0, -3.4), -9.0, -3.4),
        "skip_gain": jnp.clip(jax.random.uniform(seeds[6], (H,), jnp.float32, 0.5, 1.5), 0.5, 1.5),
        "dt_bias": jnp.clip(jax.random.uniform(seeds[7], (H,), jnp.float32, -0.5, 0.5), -0.5, 0.5),
        "out_grad": bell_draw(seeds[8], (ROLLS, SEQ, H * P_SIZE), 1.0, 6.0, ((0, 4), (1, 32))),
    }


def decay_terms(dt_raw, starts, a_log, dt_bias):
    dt_step = jax.nn.softplus(dt_raw + dt_bias[None, :])
    decay_rate = -jnp.exp(a_log)
    cum_decay = jnp.cumsum(dt_step * decay_rate[None, :], axis=0)
    span_count = jnp.cumsum(starts, axis=0)
    return (dt_step, cum_decay, span_count)

def stretch_summary(x_rows, b_rows, dt_raw, starts, a_log, dt_bias):
    dt_step, cum_decay, span_count = decay_terms(dt_raw, starts, a_log, dt_bias)
    length = x_rows.shape[0]
    heads_per = H // G
    kept_rows = jnp.where(span_count == span_count[length - 1], 1.0, 0.0)
    weight = jnp.exp(cum_decay[length - 1][None, :] - cum_decay) * dt_step * kept_rows[:, None]
    carried = jnp.where(span_count[length - 1] == 0, jnp.exp(cum_decay[length - 1]), 0.0 * cum_decay[length - 1])
    scaled = x_rows.reshape(length, G, heads_per, P_SIZE) * weight.reshape(length, G, heads_per)[..., None]
    state_sum = jnp.einsum('tgkp,tgn->gkpn', scaled, b_rows.reshape(length, G, N), precision=lax.Precision.HIGHEST)
    return (carried, state_sum.reshape(H, P_SIZE, N))

def state_reach(c_rows, cum_decay, span_count):
    length = c_rows.shape[0]
    heads_per = H // G
    enters = jnp.where(span_count == 0, 1.0, 0.0)
    carry_reach = jnp.exp(cum_decay) * enters[:, None]
    return c_rows.reshape(length, G, 1, N) * carry_reach.reshape(length, G, heads_per, 1)

def stretch_output(x_rows, b_rows, c_rows, dt_raw, starts, state_in, a_log, skip_gain, dt_bias):
    dt_step, cum_decay, span_count = decay_terms(dt_raw, starts, a_log, dt_bias)
    length = x_rows.shape[0]
    heads_per = H // G
    x_half = x_rows.astype(jnp.bfloat16)
    b_half = b_rows.astype(jnp.bfloat16)
    c_half = c_rows.astype(jnp.bfloat16)
    scores = jnp.einsum('tgn,sgn->gts', c_half.reshape(length, G, N), b_half.reshape(length, G, N), preferred_element_type=jnp.float32)
    position = jnp.arange(length)
    visible = (position[:, None] >= position[None, :]) & (span_count[:, None] == span_count[None, :])
    seen = visible[None, None]
    cum_heads = jnp.transpose(cum_decay).reshape(G, heads_per, length)
    dt_heads = jnp.transpose(dt_step).reshape(G, heads_per, length)
    log_gap = cum_heads[:, :, :, None] - cum_heads[:, :, None, :]
    log_gap = jnp.where(seen, log_gap, 0.0)
    factor = jnp.exp(log_gap) * jnp.where(seen, 1.0, 0.0) * dt_heads[:, :, None, :]
    mixing = (scores[:, None] * factor).astype(jnp.bfloat16)
    within = jnp.einsum('gkts,sgkp->tgkp', mixing, x_half.reshape(length, G, heads_per, P_SIZE), preferred_element_type=jnp.float32)
    weighted_c = state_reach(c_rows, cum_decay, span_count)
    from_state = jnp.einsum('tgkn,gkpn->tgkp', weighted_c, state_in.reshape(G, heads_per, P_SIZE, N), precision=lax.Precision.HIGHEST)
    skip_part = x_rows.reshape(length, G, heads_per, P_SIZE) * skip_gain.reshape(G, heads_per)[None, :, :, None]
    return (within + from_state + skip_part).reshape(length, H * P_SIZE).astype(jnp.bfloat16)

def unfold(array):
    shaped = array.reshape((N_DP, N_CTX, 2, STRETCH) + array.shape[2:])
    early = shaped[:, :, 0]
    late = jnp.flip(shaped[:, :, 1], axis=1)
    return jnp.concatenate([early, late], axis=1)

def refold(array):
    early = array[:, :N_CTX]
    late = jnp.flip(array[:, N_CTX:], axis=1)
    return jnp.stack([early, late], axis=2).reshape((N_DP, SEQ) + array.shape[3:])

def replica_pass(pieces, a_log, skip_gain, dt_bias):
    x_all, b_all, c_all, dt_all, start_all, grad_all = pieces

    def forward(x_all, b_all, c_all, dt_all, a_log, skip_gain, dt_bias):

        def advance(state_now, block):
            x_rows, b_rows, c_rows, dt_rows, start_rows = block
            carried, local_sum = stretch_summary(x_rows, b_rows, dt_rows, start_rows, a_log, dt_bias)
            out_rows = stretch_output(x_rows, b_rows, c_rows, dt_rows, start_rows, state_now, a_log, skip_gain, dt_bias)
            return (carried[:, None, None] * state_now + local_sum, out_rows)
        initial = jnp.zeros((H, P_SIZE, N), jnp.float32)
        final_state, outputs = lax.scan(jax.checkpoint(advance), initial, (x_all, b_all, c_all, dt_all, start_all))
        return outputs
    outputs, pullback = jax.vjp(forward, x_all, b_all, c_all, dt_all, a_log, skip_gain, dt_bias)
    gradients = pullback(grad_all)
    return (outputs,) + tuple(gradients)

def reference(hidden_x, b_proj, c_proj, dt_raw, span_start, a_log, skip_gain, dt_bias, out_grad):
    pieces = (unfold(hidden_x.astype(jnp.float32)), unfold(b_proj.astype(jnp.float32)), unfold(c_proj.astype(jnp.float32)), unfold(dt_raw), unfold(span_start), unfold(out_grad))

    def one_replica(replica):
        return replica_pass(replica, a_log, skip_gain, dt_bias)
    results = lax.map(one_replica, pieces)
    outputs, grad_xs, grad_bs, grad_cs, grad_dts, grad_as, grad_ks, grad_ts = results
    return (refold(outputs), refold(grad_xs).astype(jnp.bfloat16), refold(grad_bs).astype(jnp.bfloat16), refold(grad_cs).astype(jnp.bfloat16), refold(grad_dts), lax.optimization_barrier(jnp.sum(grad_as, axis=0)), lax.optimization_barrier(jnp.sum(grad_ks, axis=0)), lax.optimization_barrier(jnp.sum(grad_ts, axis=0)))
```

```python
import functools

import jax
import jax.numpy as jnp
from jax import lax
from jax.experimental import pallas as pl
from jax.experimental.pallas import tpu as pltpu
from jax.sharding import PartitionSpec as P

H = 64
P_SIZE = 32
N = 64
G = 4
STRETCH = 256
ROWS = 2 * STRETCH
WIDTH = H * P_SIZE
GROUP = WIDTH // G
STEPS = 2
STEP_W = WIDTH // STEPS
STEP_N = G * N // STEPS
XY = 16
LANES = WIDTH // XY
CHUNKS = 4
CH = N // CHUNKS
F32 = jnp.float32
BF16 = jnp.bfloat16
MESH = pl.DeviceIdType.MESH
NN = ((1,), (0,))
NT = ((1,), (1,))
TN = ((0,), (0,))


def dot(a, b, dims=NN, precision=None):
    return lax.dot_general(a, b, (dims, ((), ())), preferred_element_type=F32, precision=precision)


def split(a):
    high = a.astype(BF16)
    return high, (a - high.astype(F32)).astype(BF16)


def head_map(step):
    head = lax.broadcasted_iota(jnp.int32, (H, STEP_W), 0)
    column = lax.broadcasted_iota(jnp.int32, (H, STEP_W), 1) + step * STEP_W
    return jnp.where(column // P_SIZE == head, 1.0, 0.0).astype(BF16)


def triangle(lower):
    row = lax.broadcasted_iota(jnp.int32, (STRETCH, STRETCH), 0)
    column = lax.broadcasted_iota(jnp.int32, (STRETCH, STRETCH), 1)
    return jnp.where(row >= column if lower else row <= column, 1.0, 0.0)


def decay_terms(dt_raw, a_log, dt_bias):
    shifted = dt_raw + dt_bias
    small = jnp.exp(-jnp.abs(shifted))
    dt = jnp.maximum(shifted, 0.0) + jnp.log1p(small)
    running = dot(triangle(True), dt, precision=lax.Precision.HIGHEST)
    return shifted, dt, -jnp.exp(a_log) * running


def counts(start_row):
    start = jnp.broadcast_to(start_row.astype(F32), (8, STRETCH)).astype(BF16)
    low = triangle(True).astype(BF16)
    return dot(low, start, NT)[:, :1], dot(start, low, NT)[:1]


def summary_kernel(x_ref, go_ref, b_ref, c_ref, dt_ref, start_ref, al_ref, tb_ref, part_ref, decay_ref, u_s, v_s, m_s):
    step = pl.program_id(0)

    @pl.when(step == 0)
    def _():
        for block in range(2):
            rows = pl.ds(block * STRETCH, STRETCH)
            _, dt, cum = decay_terms(dt_ref[rows], al_ref[...], tb_ref[...])
            u_s[rows] = jnp.concatenate(split(jnp.exp(cum)), axis=1)
            v_s[rows] = jnp.concatenate(split(jnp.exp(-cum) * dt), axis=1)
            column, _ = counts(start_ref[:, block * STRETCH : (block + 1) * STRETCH])
            last = column[STRETCH - 1 :]
            enters = jnp.where(column == 0.0, 1.0, 0.0)
            stays = jnp.where(column == last, 1.0, 0.0)
            m_s[rows] = jnp.concatenate(
                [jnp.broadcast_to(enters, (STRETCH, N)), jnp.broadcast_to(stays, (STRETCH, N))], axis=1
            )

    heads = head_map(step)
    heads = jnp.concatenate([heads, heads], axis=0)
    decays = []
    for block in range(2):
        rows = pl.ds(block * STRETCH, STRETCH)
        mask = m_s[rows]
        enters, stays = mask[:, :N], mask[:, N:]
        for group in range(G // STEPS):
            cols = pl.ds(group * GROUP, GROUP)
            expand = heads[:, group * GROUP : (group + 1) * GROUP]
            u = dot(u_s[rows], expand)
            v = dot(v_s[rows], expand)
            total = u[STRETCH - 1 :]
            scaled_x = (x_ref[rows, cols].astype(F32) * (v * total)).astype(BF16)
            scaled_g = (go_ref[rows, cols].astype(F32) * u).astype(BF16)
            b_in = b_ref[rows, group * N : (group + 1) * N]
            c_in = c_ref[rows, group * N : (group + 1) * N]
            b_in = (b_in.astype(F32) * stays).astype(BF16)
            c_in = (c_in.astype(F32) * enters).astype(BF16)
            part_ref[0, block, :, cols] = dot(b_in, scaled_x, TN)
            part_ref[1, 1 - block, :, cols] = dot(c_in, scaled_g, TN)
            kept = jnp.broadcast_to(enters[STRETCH - 1 :, :1], (1, GROUP))
            decays.append(total * kept)
    first = jnp.concatenate(decays[: G // STEPS], axis=1)
    second = jnp.concatenate(decays[G // STEPS :], axis=1)
    row = lax.broadcasted_iota(jnp.int32, (8, STEP_W), 0)
    decay_ref[...] = jnp.where(row == 0, first, jnp.where(row == 1, second, 0.0))


def chain_kernel(part, decay, state, z_in, z_decay, up, up_in, down, down_in, z_out, z_s, z_r, up_s, up_r, down_s, down_r, back_s, back_r):
    here = lax.axis_index("ctx")
    side, place = lax.rem(here, 2), here // 2
    partner = {"ctx": here + 1 - 2 * side}

    def peer(k):
        return lax.rem(place + k, XY)

    def device(k):
        return {"ctx": peer(k) * 2 + side}

    barrier = pltpu.get_barrier_semaphore()
    pl.semaphore_signal(barrier, inc=1, device_id=partner, device_id_type=MESH)

    def greet(k, carry):
        pl.semaphore_signal(barrier, inc=1, device_id=device(k), device_id_type=MESH)
        return carry

    lax.fori_loop(1, XY, greet, 0)
    pl.semaphore_wait(barrier, XY)

    def remote(src, dst, send, recv, to):
        return pltpu.make_async_remote_copy(
            src_ref=src, dst_ref=dst, send_sem=send, recv_sem=recv, device_id=to, device_id_type=MESH
        )

    def z_up(q):
        rows = pl.ds(q * CH, CH)
        return remote(part.at[1 - side, :, rows], z_in.at[:, rows], z_s.at[q], z_r.at[q], partner)

    z_decays = remote(decay, z_decay, z_s.at[CHUNKS], z_r.at[CHUNKS], partner)
    z_decays.start()
    for q in range(CHUNKS):
        z_up(q).start()

    def up_rows(q):
        return pl.ds(8 + q * 2 * CH, 2 * CH) if q else pl.ds(0, 8 + 2 * CH)

    def up_copy(q, k):
        return remote(up.at[peer(k), up_rows(q)], up_in.at[place, up_rows(q)], up_s.at[q, k], up_r.at[q, k], device(k))

    def down_rows(q):
        return pl.ds(q * 2 * CH, 2 * CH)

    def down_copy(q, k):
        return remote(down.at[peer(k), down_rows(q)], down_in.at[place, down_rows(q)], down_s.at[q, k], down_r.at[q, k], device(k))

    def z_back(q):
        rows = pl.ds(q * CH, CH)
        return remote(z_out.at[:, rows], state.at[side, :, rows], back_s.at[q], back_r.at[q], partner)

    z_decays.wait_recv()
    at_zero = side == 0
    mine = [jnp.where(at_zero, decay[s : s + 1], decay[1 - s : 2 - s]) for s in range(2)]
    theirs = [jnp.where(at_zero, z_decay[s : s + 1], z_decay[1 - s : 2 - s]) for s in range(2)]
    first = [at_zero, jnp.logical_not(at_zero)]

    for q in range(CHUNKS):
        rows = pl.ds(q * CH, CH)
        z_up(q).wait_recv()
        if q == 0:
            pair = [mine[s] * theirs[s] for s in range(2)]
            row = lax.broadcasted_iota(jnp.int32, (8, LANES), 0)
            for o in range(XY):
                lanes = slice(o * LANES, (o + 1) * LANES)
                up[o, :8] = jnp.where(row == 0, pair[0][:, lanes], jnp.where(row == 1, pair[1][:, lanes], 0.0))
        for s in range(2):
            scale_mine = jnp.where(first[s], theirs[s], 1.0)
            scale_theirs = jnp.where(first[s], 1.0, mine[s])
            total = scale_mine * part[side, s, rows] + scale_theirs * z_in[s, rows]
            for o in range(XY):
                up[o, pl.ds(8 + (2 * q + s) * CH, CH)] = total[:, o * LANES : (o + 1) * LANES]

        def send_up(k, carry):
            up_copy(q, k).start()
            return carry

        lax.fori_loop(1, XY, send_up, 0)
        up_in[place, up_rows(q)] = up[place, up_rows(q)]

    for q in range(CHUNKS):

        def await_up(k, carry):
            up_copy(q, k).wait_recv()
            return carry

        lax.fori_loop(1, XY, await_up, 0)

        def rise(j, now):
            down[j, pl.ds(2 * q * CH, CH)] = now
            return up_in[j, 0:1] * now + up_in[j, pl.ds(8 + 2 * q * CH, CH)]

        def fall(k, now):
            j = XY - 1 - k
            down[j, pl.ds((2 * q + 1) * CH, CH)] = now
            return up_in[j, 1:2] * now + up_in[j, pl.ds(8 + (2 * q + 1) * CH, CH)]

        now = lax.fori_loop(0, XY, rise, jnp.zeros((CH, LANES), F32))
        lax.fori_loop(0, XY, fall, now)

        def send_down(k, carry):
            down_copy(q, k).start()
            return carry

        lax.fori_loop(1, XY, send_down, 0)
        down_in[place, down_rows(q)] = down[place, down_rows(q)]

    for q in range(CHUNKS):
        rows = pl.ds(q * CH, CH)

        def await_down(k, carry):
            down_copy(q, k).wait_recv()
            return carry

        lax.fori_loop(1, XY, await_down, 0)
        for s in range(2):
            keep = jnp.where(first[s], 1.0, theirs[s])
            keep_add = jnp.where(first[s], 0.0, 1.0)
            give = jnp.where(first[s], mine[s], 1.0)
            give_add = jnp.where(first[s], 1.0, 0.0)
            enter = jnp.concatenate([down_in[o, pl.ds((2 * q + s) * CH, CH)] for o in range(XY)], axis=1)
            state[side, s, rows] = keep * enter + keep_add * z_in[s, rows]
            z_out[s, rows] = give * enter + give_add * part[side, s, rows]
        z_back(q).start()

    for q in range(CHUNKS):
        z_back(q).wait()
        z_up(q).wait_send()

        def await_sent(k, carry):
            up_copy(q, k).wait_send()
            down_copy(q, k).wait_send()
            return carry

        lax.fori_loop(1, XY, await_sent, 0)
    z_decays.wait_send()


def output_kernel(x_ref, go_ref, b_ref, c_ref, dt_ref, start_ref, al_ref, sk_ref, tb_ref, state_ref, mixed_ref, gx_ref, gb_ref, gc_ref, gdt_ref, params_ref, u_s, v_s, m_s, cum_s, seen_s, seen_t, net_s, late_s, end_s, skip_s):
    step = pl.program_id(0)

    @pl.when(step == 0)
    def _():
        for block in range(2):
            rows = pl.ds(block * STRETCH, STRETCH)
            _, dt, cum = decay_terms(dt_ref[rows], al_ref[...], tb_ref[...])
            cum_s[rows] = cum
            u_s[rows] = jnp.concatenate(split(jnp.exp(cum)), axis=1)
            v_s[rows] = jnp.concatenate(split(jnp.exp(-cum) * dt), axis=1)
            column, row = counts(start_ref[:, block * STRETCH : (block + 1) * STRETCH])
            last = column[STRETCH - 1 :]
            enters = jnp.where(column == 0.0, 1.0, 0.0)
            stays = jnp.where(column == last, 1.0, 0.0)
            m_s[rows] = jnp.concatenate(
                [jnp.broadcast_to(enters, (STRETCH, N)), jnp.broadcast_to(stays, (STRETCH, N))], axis=1
            )
            same = jnp.where(column == row, 1.0, 0.0)
            seen_s[rows] = same * triangle(True)
            seen_t[rows] = same * triangle(False)
        net_s[...] = jnp.zeros_like(net_s)
        late_s[...] = jnp.zeros_like(late_s)
        end_s[...] = jnp.zeros_like(end_s)
        skip_s[...] = jnp.zeros_like(skip_s)

    heads = head_map(step)
    twice = jnp.concatenate([heads, heads], axis=0)
    skip_row = dot(jnp.concatenate(split(jnp.broadcast_to(sk_ref[...], (8, H))), axis=1), twice)[:1]

    def by_head(values, where):
        high, low = split(values)
        return dot(high, where, NT) + dot(low, where, NT)

    for block in range(2):
        rows = pl.ds(block * STRETCH, STRETCH)
        mask = m_s[rows]
        enters, stays = mask[:, :N], mask[:, N:]
        seen, seen_back = seen_s[rows], seen_t[rows]
        for group in range(G // STEPS):
            cols = pl.ds(group * GROUP, GROUP)
            lanes = slice(group * GROUP, (group + 1) * GROUP)
            where = heads[:, lanes]
            expand = twice[:, lanes]
            u = dot(u_s[rows], expand)
            v = dot(v_s[rows], expand)
            total = u[STRETCH - 1 :]
            x = x_ref[rows, cols].astype(F32)
            go = go_ref[rows, cols].astype(F32)
            xv = (x * v).astype(BF16)
            gu = (go * u).astype(BF16)
            xk = (x * (v * total)).astype(BF16)
            narrow = slice(group * N, (group + 1) * N)
            b_in, c_in = b_ref[rows, narrow], c_ref[rows, narrow]
            b_stay = (b_in.astype(F32) * stays).astype(BF16)
            c_enter = (c_in.astype(F32) * enters).astype(BF16)
            entering = state_ref[0, block, :, cols]
            later = state_ref[1, 1 - block, :, cols]
            entering_half, later_half = entering.astype(BF16), later.astype(BF16)
            scores = (dot(c_in, b_in, NT) * seen).astype(BF16)
            scores_back = (dot(b_in, c_in, NT) * seen_back).astype(BF16)
            y = dot(scores, xv) + dot(c_enter, entering_half)
            from_later = total * dot(b_stay, later_half)
            z = dot(scores_back, gu) + from_later
            skip = skip_row[:, lanes]
            mixed_ref[rows, cols] = (u * y + skip * x).astype(BF16)
            gx_ref[rows, cols] = (v * z + skip * go).astype(BF16)
            grad_scores = jnp.where(seen > 0.0, dot(gu, xv, NT), 0.0).astype(BF16)
            gc_ref[rows, narrow] = (dot(grad_scores, b_in) + enters * dot(gu, entering_half, NT)).astype(BF16)
            gb_ref[rows, narrow] = (dot(grad_scores, c_in, TN) + stays * dot(xk, later_half, NT)).astype(BF16)
            xv_wide = xv.astype(F32)
            from_z = xv_wide * z
            net_s[rows] += by_head(gu.astype(F32) * y - from_z, where)
            late_s[rows] += by_head(from_z, where)
            kept = jnp.broadcast_to(enters[STRETCH - 1 :, :1], (1, GROUP))
            ends = jnp.sum(xv_wide * from_later, axis=0, keepdims=True)
            ends += total * kept * jnp.sum(entering * later, axis=0, keepdims=True)
            end_s[block * 8 : (block + 1) * 8] += by_head(jnp.broadcast_to(ends, (8, GROUP)), where)
            skips = jnp.sum(x * go, axis=0, keepdims=True)
            skip_s[...] += by_head(jnp.broadcast_to(skips, (8, GROUP)), where)

    @pl.when(step == STEPS - 1)
    def _():
        rate = -jnp.exp(al_ref[...])
        grad_a = jnp.zeros((1, H), F32)
        grad_t = jnp.zeros((1, H), F32)
        position = lax.broadcasted_iota(jnp.int32, (STRETCH, H), 0)
        for block in range(2):
            rows = pl.ds(block * STRETCH, STRETCH)
            shifted = dt_ref[rows] + tb_ref[...]
            small = jnp.exp(-jnp.abs(shifted))
            dt = jnp.maximum(shifted, 0.0) + jnp.log1p(small)
            slope = jnp.where(shifted >= 0.0, 1.0, small) / (1.0 + small)
            grad_cum = net_s[rows] + jnp.where(position == STRETCH - 1, end_s[block * 8 : block * 8 + 1], 0.0)
            after = dot(triangle(False), grad_cum, precision=lax.Precision.HIGHEST)
            grad_dt = (late_s[rows] / dt + rate * after) * slope
            gdt_ref[rows] = grad_dt
            grad_a += jnp.sum(cum_s[rows] * grad_cum, axis=0, keepdims=True)
            grad_t += jnp.sum(grad_dt, axis=0, keepdims=True)
        row = lax.broadcasted_iota(jnp.int32, (8, H), 0)
        params_ref[...] = jnp.where(row == 0, grad_a, jnp.where(row == 1, skip_s[:1], jnp.where(row == 2, grad_t, 0.0)))


def total_kernel(x, a_ref, k_ref, t_ref, buf1, buf2, s1, r1, s2, r2):
    here, dp = lax.axis_index("ctx"), lax.axis_index("dp")
    side, place = lax.rem(here, 2), here // 2
    mine = dp * 2 + side

    def near(k):
        return {"ctx": lax.rem(place + k, XY) * 2 + side}

    def far(k):
        g = lax.rem(mine + k, 8)
        return {"dp": g // 2, "ctx": place * 2 + lax.rem(g, 2)}

    barrier = pltpu.get_barrier_semaphore()
    for k in range(1, XY):
        pl.semaphore_signal(barrier, inc=1, device_id=near(k), device_id_type=MESH)
    for k in range(1, 8):
        pl.semaphore_signal(barrier, inc=1, device_id=far(k), device_id_type=MESH)
    pl.semaphore_wait(barrier, XY + 6)

    def exchange(src, buf, send, recv, to, count):
        copies = []
        for k in range(1, count):
            copy = pltpu.make_async_remote_copy(
                src_ref=src, dst_ref=buf.at[k], send_sem=send.at[k], recv_sem=recv.at[k], device_id=to(k), device_id_type=MESH
            )
            copy.start()
            copies.append(copy)
        for copy in copies:
            copy.wait()

    buf1[0] = x[...]
    exchange(x, buf1, s1, r1, near, XY)
    buf2[0] = jnp.sum(buf1[...], axis=0)
    exchange(buf2.at[0], buf2, s2, r2, far, 8)
    total = jnp.zeros((8, H), F32)
    for g in range(8):
        total += buf2[lax.rem(g - mine + 8, 8)]
    a_ref[...] = total[0:1]
    k_ref[...] = total[1:2]
    t_ref[...] = total[2:3]


def shards(hidden_x, b_proj, c_proj, dt_raw, span_start, a_log, skip_gain, dt_bias, out_grad):
    x = hidden_x.reshape(ROWS, WIDTH)
    go = out_grad.reshape(ROWS, WIDTH)
    b = b_proj.reshape(ROWS, G * N)
    c = c_proj.reshape(ROWS, G * N)
    dt = dt_raw.reshape(ROWS, H)
    start = span_start.reshape(1, ROWS)
    al, sk, tb = a_log.reshape(1, H), skip_gain.reshape(1, H), dt_bias.reshape(1, H)

    wide = pl.BlockSpec((ROWS, STEP_W), lambda i: (0, i))
    narrow = pl.BlockSpec((ROWS, STEP_N), lambda i: (0, i))

    def whole(*shape):
        return pl.BlockSpec(shape, lambda i: (0,) * len(shape))

    vmem = pl.BlockSpec(memory_space=pltpu.VMEM)
    part, decay = pl.pallas_call(
        summary_kernel,
        grid=(STEPS,),
        out_shape=(jax.ShapeDtypeStruct((2, 2, N, WIDTH), F32), jax.ShapeDtypeStruct((8, WIDTH), F32)),
        in_specs=[wide, wide, narrow, narrow, whole(ROWS, H), whole(1, ROWS), whole(1, H), whole(1, H)],
        out_specs=(
            pl.BlockSpec((2, 2, N, STEP_W), lambda i: (0, 0, 0, i)),
            pl.BlockSpec((8, STEP_W), lambda i: (0, i)),
        ),
        scratch_shapes=[
            pltpu.VMEM((ROWS, 2 * H), BF16),
            pltpu.VMEM((ROWS, 2 * H), BF16),
            pltpu.VMEM((ROWS, 2 * N), F32),
        ],
        compiler_params=pltpu.CompilerParams(vmem_limit_bytes=48 * 2**20),
        cost_estimate=pl.CostEstimate(flops=10**9, bytes_accessed=8 * 2**20, transcendentals=10**5),
        name="summary",
    )(x, go, b, c, dt, start, al, tb)

    dma = pltpu.SemaphoreType.DMA
    state = pl.pallas_call(
        chain_kernel,
        out_shape=jax.ShapeDtypeStruct((2, 2, N, WIDTH), F32),
        in_specs=[vmem, vmem],
        out_specs=vmem,
        scratch_shapes=[
            pltpu.VMEM((2, N, WIDTH), F32),
            pltpu.VMEM((8, WIDTH), F32),
            pltpu.VMEM((XY, 8 + 2 * N, LANES), F32),
            pltpu.VMEM((XY, 8 + 2 * N, LANES), F32),
            pltpu.VMEM((XY, 2 * N, LANES), F32),
            pltpu.VMEM((XY, 2 * N, LANES), F32),
            pltpu.VMEM((2, N, WIDTH), F32),
            dma((CHUNKS + 1,)),
            dma((CHUNKS + 1,)),
            dma((CHUNKS, XY)),
            dma((CHUNKS, XY)),
            dma((CHUNKS, XY)),
            dma((CHUNKS, XY)),
            dma((CHUNKS,)),
            dma((CHUNKS,)),
        ],
        compiler_params=pltpu.CompilerParams(
            collective_id=0, has_side_effects=True, vmem_limit_bytes=48 * 2**20
        ),
        name="chain",
    )(part, decay)

    half = jax.ShapeDtypeStruct((ROWS, WIDTH), BF16)
    slim = jax.ShapeDtypeStruct((ROWS, G * N), BF16)
    mixed, gx, gb, gc, gdt, params = pl.pallas_call(
        output_kernel,
        grid=(STEPS,),
        out_shape=(half, half, slim, slim, jax.ShapeDtypeStruct((ROWS, H), F32), jax.ShapeDtypeStruct((8, H), F32)),
        in_specs=[wide, wide, narrow, narrow, whole(ROWS, H), whole(1, ROWS), whole(1, H), whole(1, H), whole(1, H),
                  pl.BlockSpec((2, 2, N, STEP_W), lambda i: (0, 0, 0, i))],
        out_specs=(wide, wide, narrow, narrow, whole(ROWS, H), whole(8, H)),
        scratch_shapes=[
            pltpu.VMEM((ROWS, 2 * H), BF16),
            pltpu.VMEM((ROWS, 2 * H), BF16),
            pltpu.VMEM((ROWS, 2 * N), F32),
            pltpu.VMEM((ROWS, H), F32),
            pltpu.VMEM((ROWS, STRETCH), F32),
            pltpu.VMEM((ROWS, STRETCH), F32),
            pltpu.VMEM((ROWS, H), F32),
            pltpu.VMEM((ROWS, H), F32),
            pltpu.VMEM((16, H), F32),
            pltpu.VMEM((8, H), F32),
        ],
        compiler_params=pltpu.CompilerParams(vmem_limit_bytes=48 * 2**20),
        cost_estimate=pl.CostEstimate(flops=4 * 10**9, bytes_accessed=12 * 2**20, transcendentals=10**5),
        name="outputs",
    )(x, go, b, c, dt, start, al, sk, tb, state)

    line = jax.ShapeDtypeStruct((1, H), F32)
    grad_a, grad_k, grad_t = pl.pallas_call(
        total_kernel,
        out_shape=(line, line, line),
        in_specs=[vmem],
        out_specs=(vmem, vmem, vmem),
        scratch_shapes=[pltpu.VMEM((XY, 8, H), F32), pltpu.VMEM((8, 8, H), F32), dma((XY,)), dma((XY,)), dma((8,)), dma((8,))],
        compiler_params=pltpu.CompilerParams(collective_id=1, has_side_effects=True),
        name="totals",
    )(params)
    return (
        mixed.reshape(1, ROWS, WIDTH),
        gx.reshape(1, ROWS, WIDTH),
        gb.reshape(1, ROWS, G * N),
        gc.reshape(1, ROWS, G * N),
        gdt.reshape(1, ROWS, H),
        grad_a.reshape(H),
        grad_k.reshape(H),
        grad_t.reshape(H),
    )


def solution(mesh):
    rows = P("dp", "ctx", None)
    return jax.shard_map(
        shards,
        mesh=mesh,
        in_specs=(rows, rows, rows, rows, P("dp", "ctx"), P(), P(), P(), rows),
        out_specs=(rows, rows, rows, rows, rows, P(), P(), P()),
        check_vma=False,
    )
```

```python
import jax
import jax.numpy as jnp
from jax import lax
from jax.experimental import pallas as pl
from jax.experimental.pallas import tpu as pltpu
from jax.sharding import PartitionSpec as P

H = 64
P_SIZE = 32
N = 64
G = 4
STRETCH = 256
ROWS = 2 * STRETCH
WIDTH = H * P_SIZE
GROUP = WIDTH // G
XY = 16
LANES = 128
TILES = GROUP // LANES
BAND = N // (XY // TILES)
FAR = 8
F32 = jnp.float32
BF16 = jnp.bfloat16
MESH = pl.DeviceIdType.MESH
NN = ((1,), (0,))
NT = ((1,), (1,))
TN = ((0,), (0,))


def dot(a, b, dims=NN, precision=None):
    return lax.dot_general(a, b, (dims, ((), ())), preferred_element_type=F32, precision=precision)


def split(a):
    high = a.astype(BF16)
    return high, (a - high.astype(F32)).astype(BF16)


def triangle(lower):
    row = lax.broadcasted_iota(jnp.int32, (STRETCH, STRETCH), 0)
    column = lax.broadcasted_iota(jnp.int32, (STRETCH, STRETCH), 1)
    return jnp.where(row >= column if lower else row <= column, 1.0, 0.0)


def counts(start_row):
    start = jnp.broadcast_to(start_row.astype(F32), (8, STRETCH)).astype(BF16)
    low = triangle(True).astype(BF16)
    return dot(low, start, NT)[:, :1], dot(start, low, NT)[:1]


def layer_kernel(
    x_hbm, go_hbm, b_hbm, c_hbm, dt_hbm, start_hbm, al_hbm, sk_hbm, tb_hbm,
    mixed, gx, gb, gc, gdt, grad_a, grad_k, grad_t,
    x_v, go_v, b_v, c_v, dt_v, start_v, al, sk, tb,
    heads, dt_s, slope_s, cum_s, u_s, v_s, enter_s, stay_s, seen_s, seen_t,
    y_s, z_s, gb_s, gc_s, net_s, late_s, end_s, skip_s,
    decay, z_decay, part, state, z_in, z_out, up, up_in, down, down_in, params, buf1, buf2,
    in_sem, z_s_sem, z_r_sem, up_s_sem, up_r_sem, down_s_sem, down_r_sem, back_s_sem, back_r_sem,
    s1, r1, s2, r2,
):
    here, dp = lax.axis_index("ctx"), lax.axis_index("dp")
    side, place = lax.rem(here, 2), here // 2
    partner = {"ctx": here + 1 - 2 * side}
    mine_far = dp * 2 + side

    def peer(k):
        return lax.rem(place + k, XY)

    def near(k):
        return {"ctx": peer(k) * 2 + side}

    def far(k):
        g = lax.rem(mine_far + k, FAR)
        return {"dp": g // 2, "ctx": place * 2 + lax.rem(g, 2)}

    loads = []

    def load(src, dst):
        copy = pltpu.make_async_copy(src, dst, in_sem.at[len(loads)])
        copy.start()
        loads.append(copy)
        return copy

    def columns(g):
        return pl.ds(g * GROUP, GROUP)

    small = [load(s, d) for s, d in ((dt_hbm, dt_v), (start_hbm, start_v), (al_hbm, al), (tb_hbm, tb), (sk_hbm, sk))]
    narrow_in = [load(b_hbm, b_v), load(c_hbm, c_v)]
    wide_in = [
        [load(x_hbm.at[:, columns(g)], x_v.at[:, columns(g)]), load(go_hbm.at[:, columns(g)], go_v.at[:, columns(g)])]
        for g in range(G)
    ]

    barrier = pltpu.get_barrier_semaphore()

    def greet_near(k, carry):
        pl.semaphore_signal(barrier, inc=1, device_id=near(k), device_id_type=MESH)
        return carry

    def greet_far(k, carry):
        pl.semaphore_signal(barrier, inc=1, device_id=far(k), device_id_type=MESH)
        return carry

    lax.fori_loop(1, XY, greet_near, 0)
    lax.fori_loop(1, FAR, greet_far, 0)

    def remote(src, dst, send, recv, to):
        return pltpu.make_async_remote_copy(
            src_ref=src, dst_ref=dst, send_sem=send, recv_sem=recv, device_id=to, device_id_type=MESH
        )

    def z_up(g):
        return remote(part.at[1 - side, g], z_in.at[g], z_s_sem.at[g], z_r_sem.at[g], partner)

    def z_decays():
        return remote(decay, z_decay, z_s_sem.at[G], z_r_sem.at[G], partner)

    def up_rows(g):
        return pl.ds(8 + g * 2 * BAND, 2 * BAND) if g else pl.ds(0, 8 + 2 * BAND)

    def up_copy(g, k):
        return remote(up.at[peer(k), up_rows(g)], up_in.at[place, up_rows(g)], up_s_sem.at[g, k], up_r_sem.at[g, k], near(k))

    def down_rows(g):
        return pl.ds(g * 2 * BAND, 2 * BAND)

    def down_copy(g, k):
        return remote(down.at[peer(k), down_rows(g)], down_in.at[place, down_rows(g)], down_s_sem.at[g, k], down_r_sem.at[g, k], near(k))

    def z_back(g):
        return remote(z_out.at[g], state.at[side, g], back_s_sem.at[g], back_r_sem.at[g], partner)

    def each_peer(act):
        def body(k, carry):
            act(k)
            return carry

        lax.fori_loop(1, XY, body, 0)

    head = lax.broadcasted_iota(jnp.int32, (H, WIDTH), 0)
    column = lax.broadcasted_iota(jnp.int32, (H, WIDTH), 1)
    mapped = jnp.where(column // P_SIZE == head, 1.0, 0.0).astype(BF16)
    heads[:H] = mapped
    heads[H:] = mapped
    for copy in small:
        copy.wait()
    rate = -jnp.exp(al[...])
    lows = triangle(True)
    lasts = []
    for block in range(2):
        rows = pl.ds(block * STRETCH, STRETCH)
        shifted = jnp.transpose(dt_v[:, block * STRETCH : (block + 1) * STRETCH]) + tb[...]
        tail = jnp.exp(-jnp.abs(shifted))
        dt = jnp.maximum(shifted, 0.0) + jnp.log1p(tail)
        dt_s[rows] = dt
        slope_s[rows] = jnp.where(shifted >= 0.0, 1.0, tail) / (1.0 + tail)
        cum = rate * dot(lows, dt, precision=lax.Precision.HIGHEST)
        cum_s[rows] = cum
        u_s[rows] = jnp.concatenate(split(jnp.exp(cum)), axis=1)
        v_s[rows] = jnp.concatenate(split(jnp.exp(-cum) * dt), axis=1)
        count, count_row = counts(start_v[:, block * STRETCH : (block + 1) * STRETCH])
        enters = jnp.broadcast_to(jnp.where(count == 0.0, 1.0, 0.0), (STRETCH, N))
        enter_s[rows] = enters
        stay_s[rows] = jnp.broadcast_to(jnp.where(count == count[STRETCH - 1 :], 1.0, 0.0), (STRETCH, N))
        same = jnp.where(count == count_row, 1.0, 0.0)
        seen_s[rows] = same * lows
        seen_t[rows] = same * triangle(False)
        total = dot(u_s[pl.ds((block + 1) * STRETCH - 16, 16)], heads[...])[15:]
        lasts.append(total * jnp.where(count[STRETCH - 1 :] == 0.0, 1.0, 0.0))
    row = lax.broadcasted_iota(jnp.int32, (8, WIDTH), 0)
    decay[...] = jnp.where(row == 0, lasts[0], jnp.where(row == 1, lasts[1], 0.0))
    net_s[...] = jnp.zeros_like(net_s)
    late_s[...] = jnp.zeros_like(late_s)
    end_s[...] = jnp.zeros_like(end_s)
    skip_s[...] = jnp.zeros_like(skip_s)
    skip_row = dot(jnp.concatenate(split(jnp.broadcast_to(sk[...], (8, H))), axis=1), heads[...])[:1]

    def narrow(g):
        return slice(g * N, (g + 1) * N)

    def by_head(values, where):
        high, low = split(values)
        return dot(high, where, NT) + dot(low, where, NT)

    def twice(a, axis):
        return jnp.concatenate([a, a], axis=axis)

    def views(g, block):
        rows, cols = pl.ds(block * STRETCH, STRETCH), columns(g)
        u = dot(u_s[rows], heads[:, cols])
        v = dot(v_s[rows], heads[:, cols])
        x = x_v[rows, cols].astype(F32)
        go = go_v[rows, cols].astype(F32)
        return rows, cols, u, v, x, go

    def kept_rows(ref, mask, g, rows):
        return (ref[rows, narrow(g)].astype(F32) * mask[rows]).astype(BF16)

    def local(g):
        for copy in wide_in[g]:
            copy.wait()
        for block in range(2):
            rows, cols, u, v, x, go = views(g, block)
            xk = jnp.concatenate(split(x * (v * u[STRETCH - 1 :])), axis=0)
            gu = jnp.concatenate(split(go * u), axis=0)
            part[0, g, block] = dot(twice(kept_rows(b_v, stay_s, g, rows), 0), xk, TN)
            part[1, g, 1 - block] = dot(twice(kept_rows(c_v, enter_s, g, rows), 0), gu, TN)

    def intra(g):
        for block in range(2):
            rows, cols, u, v, x, go = views(g, block)
            b_in, c_in = b_v[rows, narrow(g)], c_v[rows, narrow(g)]
            gu, gu_low = split(go * u)
            xv, xv_low = split(x * v)
            scores, scores_low = split(dot(c_in, b_in, NT) * seen_s[rows])
            back, back_low = split(dot(b_in, c_in, NT) * seen_t[rows])
            y_s[rows, cols] = dot(scores, xv) + dot(scores, xv_low) + dot(scores_low, xv)
            z_s[rows, cols] = dot(back, gu) + dot(back, gu_low) + dot(back_low, gu)
            grad_scores = jnp.where(seen_s[rows] > 0.0, dot(gu, xv, NT), 0.0).astype(BF16)
            gc_s[rows, narrow(g)] = dot(grad_scores, b_in)
            gb_s[rows, narrow(g)] = dot(grad_scores, c_in, TN)
            skips = jnp.sum(x * go, axis=0, keepdims=True)
            skip_s[...] += by_head(jnp.broadcast_to(skips, (8, GROUP)), heads[:H, cols])

    def final_sums(g):
        for block in range(2):
            rows, cols, u, v, x, go = views(g, block)
            where = heads[:H, cols]
            entering, later = state[0, g, block], state[1, g, 1 - block]
            c_enter = twice(kept_rows(c_v, enter_s, g, rows), 1)
            b_stay = twice(kept_rows(b_v, stay_s, g, rows), 1)
            y = y_s[rows, cols] + dot(c_enter, jnp.concatenate(split(entering), axis=0))
            from_later = u[STRETCH - 1 :] * dot(b_stay, jnp.concatenate(split(later), axis=0))
            z = z_s[rows, cols] + from_later
            y_s[rows, cols] = y
            z_s[rows, cols] = z
            xv = x * v
            from_z = xv * z
            net_s[rows] += by_head(go * u * y - from_z, where)
            late_s[rows] += by_head(from_z, where)
            ends = jnp.sum(xv * from_later, axis=0, keepdims=True)
            ends += decay[block : block + 1, cols] * jnp.sum(entering * later, axis=0, keepdims=True)
            end_s[block * 8 : (block + 1) * 8] += by_head(jnp.broadcast_to(ends, (8, GROUP)), where)

    def final_out(g):
        skip = skip_row[:, g * GROUP : (g + 1) * GROUP]
        for block in range(2):
            rows, cols, u, v, x, go = views(g, block)
            mixed[rows, cols] = (u * y_s[rows, cols] + skip * x).astype(BF16)
            gx[rows, cols] = (v * z_s[rows, cols] + skip * go).astype(BF16)
            gu = (go * u).astype(BF16)
            xk = (x * (v * u[STRETCH - 1 :])).astype(BF16)
            entering, later = state[0, g, block].astype(BF16), state[1, g, 1 - block].astype(BF16)
            gc[rows, narrow(g)] = (gc_s[rows, narrow(g)] + enter_s[rows] * dot(gu, entering, NT)).astype(BF16)
            gb[rows, narrow(g)] = (gb_s[rows, narrow(g)] + stay_s[rows] * dot(xk, later, NT)).astype(BF16)

    at_zero = side == 0
    first = [at_zero, jnp.logical_not(at_zero)]

    def factors():
        mine = [jnp.where(at_zero, decay[s : s + 1], decay[1 - s : 2 - s]) for s in range(2)]
        theirs = [jnp.where(at_zero, z_decay[s : s + 1], z_decay[1 - s : 2 - s]) for s in range(2)]
        return mine, theirs

    def part_of(row, g):
        return row[:, g * GROUP : (g + 1) * GROUP]

    def combine(g):
        if g == 0:
            z_decays().wait_recv()
        z_up(g).wait_recv()
        mine, theirs = factors()
        if g == 0:
            pair = [mine[s] * theirs[s] for s in range(2)]
            for t in range(TILES):
                lines = [
                    pair[s][:, h * GROUP + t * LANES : h * GROUP + (t + 1) * LANES] for h in range(G) for s in range(2)
                ]
                lines = jnp.concatenate(lines, axis=0)
                for o in range(t, XY, TILES):
                    up[o, :8] = lines
        for s in range(2):
            scale_mine = jnp.where(first[s], part_of(theirs[s], g), 1.0)
            scale_theirs = jnp.where(first[s], 1.0, part_of(mine[s], g))
            total = scale_mine * part[side, g, s] + scale_theirs * z_in[g, s]
            for o in range(XY):
                band, t = o // TILES, o % TILES
                up[o, pl.ds(8 + (2 * g + s) * BAND, BAND)] = total[
                    band * BAND : (band + 1) * BAND, t * LANES : (t + 1) * LANES
                ]
        each_peer(lambda k: up_copy(g, k).start())
        up_in[place, up_rows(g)] = up[place, up_rows(g)]

    def scan(g):
        each_peer(lambda k: up_copy(g, k).wait_recv())

        def rise(j, now):
            down[j, pl.ds(2 * g * BAND, BAND)] = now
            return up_in[j, 2 * g : 2 * g + 1] * now + up_in[j, pl.ds(8 + 2 * g * BAND, BAND)]

        def fall(k, now):
            j = XY - 1 - k
            down[j, pl.ds((2 * g + 1) * BAND, BAND)] = now
            return up_in[j, 2 * g + 1 : 2 * g + 2] * now + up_in[j, pl.ds(8 + (2 * g + 1) * BAND, BAND)]

        now = lax.fori_loop(0, XY, rise, jnp.zeros((BAND, LANES), F32))
        lax.fori_loop(0, XY, fall, now)
        each_peer(lambda k: down_copy(g, k).start())
        down_in[place, down_rows(g)] = down[place, down_rows(g)]

    def spread(g):
        each_peer(lambda k: down_copy(g, k).wait_recv())
        mine, theirs = factors()
        for s in range(2):
            at = pl.ds((2 * g + s) * BAND, BAND)
            enter = jnp.concatenate(
                [
                    jnp.concatenate([down_in[r * TILES + t, at] for t in range(TILES)], axis=1)
                    for r in range(XY // TILES)
                ],
                axis=0,
            )
            keep = jnp.where(first[s], 1.0, part_of(theirs[s], g))
            keep_add = jnp.where(first[s], 0.0, 1.0)
            give = jnp.where(first[s], part_of(mine[s], g), 1.0)
            give_add = jnp.where(first[s], 1.0, 0.0)
            z_out[g, s] = give * enter + give_add * part[side, g, s]
            state[side, g, s] = keep * enter + keep_add * z_in[g, s]
        z_back(g).start()

    for copy in narrow_in:
        copy.wait()
    for g in range(G):
        local(g)
        if g == 0:
            pl.semaphore_wait(barrier, XY + FAR - 2)
            z_decays().start()
        z_up(g).start()
    for g in range(G):
        intra(g)
        combine(g)
        if g >= 1:
            scan(g - 1)
        if g >= 2:
            spread(g - 2)
    scan(G - 1)
    spread(G - 2)
    z_back(0).wait_recv()
    final_sums(0)
    spread(G - 1)
    final_out(0)
    for g in range(1, G):
        z_back(g).wait_recv()
        final_sums(g)
        if g < G - 1:
            final_out(g)

    sum_a = jnp.zeros((1, H), F32)
    sum_t = jnp.zeros((1, H), F32)
    position = lax.broadcasted_iota(jnp.int32, (STRETCH, H), 0)
    for block in range(2):
        rows = pl.ds(block * STRETCH, STRETCH)
        grad_cum = net_s[rows] + jnp.where(position == STRETCH - 1, end_s[block * 8 : block * 8 + 1], 0.0)
        after = dot(triangle(False), grad_cum, precision=lax.Precision.HIGHEST)
        grad_dt = (late_s[rows] / dt_s[rows] + rate * after) * slope_s[rows]
        gdt[:, block * STRETCH : (block + 1) * STRETCH] = jnp.transpose(grad_dt)
        sum_a += jnp.sum(cum_s[rows] * grad_cum, axis=0, keepdims=True)
        sum_t += jnp.sum(grad_dt, axis=0, keepdims=True)
    row = lax.broadcasted_iota(jnp.int32, (8, H), 0)
    params[...] = jnp.where(row == 0, sum_a, jnp.where(row == 1, skip_s[:1], jnp.where(row == 2, sum_t, 0.0)))

    def sum1(k):
        return remote(params, buf1.at[k], s1.at[k], r1.at[k], near(k))

    def sum2(k):
        return remote(buf2.at[0], buf2.at[k], s2.at[k], r2.at[k], far(k))

    def each_far(act):
        def body(k, carry):
            act(k)
            return carry

        lax.fori_loop(1, FAR, body, 0)

    each_peer(lambda k: sum1(k).start())
    buf1[0] = params[...]
    final_out(G - 1)
    for g in range(G):
        z_back(g).wait_send()
        z_up(g).wait_send()
        each_peer(lambda k: up_copy(g, k).wait_send())
        each_peer(lambda k: down_copy(g, k).wait_send())
    z_decays().wait_send()
    each_peer(lambda k: sum1(k).wait_recv())
    buf2[0] = jnp.sum(buf1[...], axis=0)
    each_far(lambda k: sum2(k).start())
    each_peer(lambda k: sum1(k).wait_send())
    each_far(lambda k: sum2(k).wait_recv())
    total = jnp.zeros((8, H), F32)
    for g in range(FAR):
        total += buf2[lax.rem(g - mine_far + FAR, FAR)]
    grad_a[...] = total[0:1]
    grad_k[...] = total[1:2]
    grad_t[...] = total[2:3]
    each_far(lambda k: sum2(k).wait_send())


def store_kernel(*refs):
    count = len(refs) // 2
    sems = refs[-1]
    copies = [pltpu.make_async_copy(refs[i], refs[count + i], sems.at[i]) for i in range(count)]
    for copy in copies:
        copy.start()
    for copy in copies:
        copy.wait()


def shards(hidden_x, b_proj, c_proj, dt_raw, span_start, a_log, skip_gain, dt_bias, out_grad):
    arrays = (
        hidden_x.reshape(ROWS, WIDTH),
        out_grad.reshape(ROWS, WIDTH),
        b_proj.reshape(ROWS, G * N),
        c_proj.reshape(ROWS, G * N),
        dt_raw.reshape(ROWS, H).T,
        span_start.reshape(1, ROWS),
        a_log.reshape(1, H),
        skip_gain.reshape(1, H),
        dt_bias.reshape(1, H),
    )
    anywhere = pl.BlockSpec(memory_space=pltpu.HBM)
    vmem = pl.BlockSpec(memory_space=pltpu.VMEM)
    dma = pltpu.SemaphoreType.DMA

    def f32(*shape):
        return pltpu.VMEM(shape, F32)

    def bf16(*shape):
        return pltpu.VMEM(shape, BF16)

    wide = jax.ShapeDtypeStruct((ROWS, WIDTH), BF16)
    slim = jax.ShapeDtypeStruct((ROWS, G * N), BF16)
    line = jax.ShapeDtypeStruct((1, H), F32)
    outs = (wide, wide, slim, slim, jax.ShapeDtypeStruct((H, ROWS), F32), line, line, line)
    held = tuple(pltpu.VMEM(out.shape, out.dtype) for out in outs)
    arrays = [pltpu.with_memory_space_constraint(a, pltpu.HBM) for a in arrays]
    results = pl.pallas_call(
        layer_kernel,
        out_shape=held,
        in_specs=[anywhere] * len(arrays),
        out_specs=(vmem,) * len(outs),
        scratch_shapes=[
            bf16(ROWS, WIDTH), bf16(ROWS, WIDTH), bf16(ROWS, G * N), bf16(ROWS, G * N), f32(H, ROWS),
            pltpu.VMEM((1, ROWS), jnp.int32), f32(1, H), f32(1, H), f32(1, H),
            bf16(2 * H, WIDTH), f32(ROWS, H), f32(ROWS, H), f32(ROWS, H), bf16(ROWS, 2 * H), bf16(ROWS, 2 * H),
            f32(ROWS, N), f32(ROWS, N), f32(ROWS, STRETCH), f32(ROWS, STRETCH),
            f32(ROWS, WIDTH), f32(ROWS, WIDTH),
            f32(ROWS, G * N), f32(ROWS, G * N), f32(ROWS, H), f32(ROWS, H), f32(16, H), f32(8, H),
            f32(8, WIDTH), f32(8, WIDTH),
            f32(2, G, 2, N, GROUP), f32(2, G, 2, N, GROUP), f32(G, 2, N, GROUP), f32(G, 2, N, GROUP),
            f32(XY, 8 + 2 * N, LANES), f32(XY, 8 + 2 * N, LANES), f32(XY, 2 * N, LANES), f32(XY, 2 * N, LANES),
            f32(8, H), f32(XY, 8, H), f32(FAR, 8, H),
            dma((7 + 2 * G,)), dma((G + 1,)), dma((G + 1,)),
            dma((G, XY)), dma((G, XY)), dma((G, XY)), dma((G, XY)), dma((G,)), dma((G,)),
            dma((XY,)), dma((XY,)), dma((FAR,)), dma((FAR,)),
        ],
        compiler_params=pltpu.CompilerParams(
            collective_id=0, has_side_effects=True, vmem_limit_bytes=44 * 2**20
        ),
        cost_estimate=pl.CostEstimate(flops=5 * 10**9, bytes_accessed=10 * 2**20, transcendentals=10**5),
        name="layer",
    )(*arrays)
    mixed, gx, gb, gc, gdt, grad_a, grad_k, grad_t = pl.pallas_call(
        store_kernel,
        out_shape=outs,
        in_specs=[vmem] * len(outs),
        out_specs=(anywhere,) * len(outs),
        scratch_shapes=[dma((len(outs),))],
        compiler_params=pltpu.CompilerParams(vmem_limit_bytes=2**20),
        name="store",
    )(*[pltpu.with_memory_space_constraint(r, pltpu.VMEM) for r in results])
    return (
        mixed.reshape(1, ROWS, WIDTH),
        gx.reshape(1, ROWS, WIDTH),
        gb.reshape(1, ROWS, G * N),
        gc.reshape(1, ROWS, G * N),
        gdt.T.reshape(1, ROWS, H),
        grad_a.reshape(H),
        grad_k.reshape(H),
        grad_t.reshape(H),
    )


def solution(mesh):
    rows = P("dp", "ctx", None)
    return jax.shard_map(
        shards,
        mesh=mesh,
        in_specs=(rows, rows, rows, rows, P("dp", "ctx"), P(), P(), P(), rows),
        out_specs=(rows, rows, rows, rows, rows, P(), P(), P()),
        check_vma=False,
    )
```

```python
import jax
import jax.numpy as jnp
from jax import lax
from jax.experimental import pallas as pl
from jax.experimental.pallas import tpu as pltpu
from jax.sharding import PartitionSpec as P

H = 64
P_SIZE = 32
N = 64
G = 4
STRETCH = 256
ROWS = 2 * STRETCH
WIDTH = H * P_SIZE
GROUP = WIDTH // G
XY = 16
LANES = 128
TILES = GROUP // LANES
BAND = N // (XY // TILES)
FAR = 8
PIECES = 4
F32 = jnp.float32
BF16 = jnp.bfloat16
MESH = pl.DeviceIdType.MESH
NN = ((1,), (0,))
NT = ((1,), (1,))
TN = ((0,), (0,))


def dot(a, b, dims=NN, precision=None):
    return lax.dot_general(a, b, (dims, ((), ())), preferred_element_type=F32, precision=precision)


def split(a):
    high = a.astype(BF16)
    return high, (a - high.astype(F32)).astype(BF16)


def triangle(lower):
    row = lax.broadcasted_iota(jnp.int32, (STRETCH, STRETCH), 0)
    column = lax.broadcasted_iota(jnp.int32, (STRETCH, STRETCH), 1)
    return jnp.where(row >= column if lower else row <= column, 1.0, 0.0)


def layer_kernel(
    x_hbm, go_hbm, b_hbm, c_hbm, dt_hbm, start_hbm, al_hbm, sk_hbm, tb_hbm,
    mixed, gx, gb, gc, gdt, grad_a, grad_k, grad_t,
    wide, b_v, c_v, dt_v, start_v, al, sk, tb,
    heads, dt_s, slope_s, cum_s, factor, v_s, masked, enter_s, stay_s, seen_s, seen_t,
    y_s, z_s, gb_s, gc_s, net_s, late_s, end_s, skip_s, weigh_s, ahead_s, early_s,
    ends_here, ends_there, decay, z_decay, part, state, z_in, z_out, up, up_in, down, down_in, params, buf1, buf2,
    in_sem, z_s_sem, z_r_sem, up_s_sem, up_r_sem, down_s_sem, down_r_sem, back_s_sem, back_r_sem,
    s1, r1, s2, r2,
):
    here, dp = lax.axis_index("ctx"), lax.axis_index("dp")
    side, place = lax.rem(here, 2), here // 2
    partner = {"ctx": here + 1 - 2 * side}
    mine_far = dp * 2 + side

    def peer(k):
        return lax.rem(place + k, XY)

    def near(k):
        return {"ctx": peer(k) * 2 + side}

    def far(k):
        g = lax.rem(mine_far + k, FAR)
        return {"dp": g // 2, "ctx": place * 2 + lax.rem(g, 2)}

    loads = []

    def load(src, dst):
        copy = pltpu.make_async_copy(src, dst, in_sem.at[len(loads)])
        copy.start()
        loads.append(copy)
        return copy

    def columns(g):
        return pl.ds(g * GROUP, GROUP)

    small = [load(s, d) for s, d in ((dt_hbm, dt_v), (start_hbm, start_v), (al_hbm, al), (tb_hbm, tb), (sk_hbm, sk))]
    narrow_in = [load(b_hbm, b_v), load(c_hbm, c_v)]
    wide_in = [
        [load(x_hbm.at[:, columns(g)], wide.at[0, :, columns(g)]), load(go_hbm.at[:, columns(g)], wide.at[1, :, columns(g)])]
        for g in range(G)
    ]

    barrier = pltpu.get_barrier_semaphore()

    def greet_near(k, carry):
        pl.semaphore_signal(barrier, inc=1, device_id=near(k), device_id_type=MESH)
        return carry

    def greet_far(k, carry):
        pl.semaphore_signal(barrier, inc=1, device_id=far(k), device_id_type=MESH)
        return carry

    lax.fori_loop(1, XY, greet_near, 0)
    lax.fori_loop(1, FAR, greet_far, 0)

    def remote(src, dst, send, recv, to):
        return pltpu.make_async_remote_copy(
            src_ref=src, dst_ref=dst, send_sem=send, recv_sem=recv, device_id=to, device_id_type=MESH
        )

    def z_up(g):
        return remote(part.at[1 - side, g], z_in.at[g], z_s_sem.at[g], z_r_sem.at[g], partner)

    def z_decays():
        return remote(ends_here, ends_there, z_s_sem.at[G], z_r_sem.at[G], partner)

    def up_rows(g):
        return pl.ds(8 + g * 2 * BAND, 2 * BAND) if g else pl.ds(0, 8 + 2 * BAND)

    def up_copy(g, k):
        return remote(up.at[peer(k), up_rows(g)], up_in.at[place, up_rows(g)], up_s_sem.at[g, k], up_r_sem.at[g, k], near(k))

    def down_rows(g):
        return pl.ds(g * 2 * BAND, 2 * BAND)

    def down_copy(g, k):
        return remote(down.at[peer(k), down_rows(g)], down_in.at[place, down_rows(g)], down_s_sem.at[g, k], down_r_sem.at[g, k], near(k))

    def z_back(g):
        return remote(z_out.at[g], state.at[side, g], back_s_sem.at[g], back_r_sem.at[g], partner)

    def each_peer(act):
        def body(k, carry):
            act(k)
            return carry

        lax.fori_loop(1, XY, body, 0)

    def map_heads(g):
        head = lax.broadcasted_iota(jnp.int32, (H, GROUP), 0)
        column = lax.broadcasted_iota(jnp.int32, (H, GROUP), 1) + g * GROUP
        mapped = jnp.where(column // P_SIZE == head, 1.0, 0.0).astype(BF16)
        heads[:H, columns(g)] = mapped
        heads[H:, columns(g)] = mapped

    def expand(values):
        return dot(jnp.concatenate(split(values), axis=1), heads[...])

    map_heads(0)
    lows = triangle(True)
    lows_half = lows.astype(BF16)
    for copy in small + narrow_in:
        copy.wait()
    rate = -jnp.exp(al[...])
    lasts, spans = [], []
    for block in range(2):
        rows = pl.ds(block * STRETCH, STRETCH)
        shifted = jnp.transpose(dt_v[:, block * STRETCH : (block + 1) * STRETCH]) + tb[...]
        tail = jnp.exp(-jnp.abs(shifted))
        dt = jnp.maximum(shifted, 0.0) + jnp.log1p(tail)
        dt_s[rows] = dt
        slope_s[rows] = jnp.where(shifted >= 0.0, 1.0, tail) / (1.0 + tail)
        dt_high, dt_rest = split(dt)
        dt_low = (dt - dt_high.astype(F32) - dt_rest.astype(F32)).astype(BF16)
        cum = rate * (dot(lows_half, dt_high) + dot(lows_half, dt_rest) + dot(lows_half, dt_low))
        cum_s[rows] = cum
        last = cum[STRETCH - 1 :]
        factor[0, rows] = jnp.concatenate(split(jnp.exp(last - cum) * dt), axis=1)
        factor[1, rows] = jnp.concatenate(split(jnp.exp(cum)), axis=1)
        v_s[rows] = jnp.concatenate(split(jnp.exp(-cum) * dt), axis=1)
        start = jnp.broadcast_to(start_v[:, block * STRETCH : (block + 1) * STRETCH].astype(F32), (8, STRETCH))
        start = start.astype(BF16)
        count = dot(lows_half, start, NT)[:, :1]
        spans.append((count, start))
        enters = jnp.where(count == 0.0, 1.0, 0.0)
        stays = jnp.where(count == count[STRETCH - 1 :], 1.0, 0.0)
        masked[0, rows] = (b_v[rows].astype(F32) * stays).astype(BF16)
        masked[1, rows] = (c_v[rows].astype(F32) * enters).astype(BF16)
        enter_s[rows] = jnp.broadcast_to(enters, (STRETCH, N))
        stay_s[rows] = jnp.broadcast_to(stays, (STRETCH, N))
        lasts.append(jnp.exp(last) * jnp.where(count[STRETCH - 1 :] == 0.0, 1.0, 0.0))
    row = lax.broadcasted_iota(jnp.int32, (8, H), 0)
    ends_here[...] = jnp.where(row == 0, lasts[0], jnp.where(row == 1, lasts[1], 0.0))

    def prepare():
        for g in range(1, G):
            map_heads(g)
        for block in range(2):
            rows = pl.ds(block * STRETCH, STRETCH)
            count, start = spans[block]
            same = jnp.where(count == dot(start, lows_half, NT)[:1], 1.0, 0.0)
            seen_s[rows] = same * lows
            seen_t[rows] = same * triangle(False)
        decay[...] = expand(ends_here[...])
        net_s[...] = jnp.zeros_like(net_s)
        late_s[...] = jnp.zeros_like(late_s)
        end_s[...] = jnp.zeros_like(end_s)
        skip_s[...] = jnp.zeros_like(skip_s)

    def narrow(g):
        return slice(g * N, (g + 1) * N)

    def by_head(values, where):
        high, low = split(values)
        return dot(high, where, NT) + dot(low, where, NT)

    def twice(a, axis):
        return jnp.concatenate([a, a], axis=axis)

    def views(g, block):
        rows, cols = pl.ds(block * STRETCH, STRETCH), columns(g)
        u = dot(factor[1, rows], heads[:, cols])
        v = dot(v_s[rows], heads[:, cols])
        x = wide[0, rows, cols].astype(F32)
        go = wide[1, rows, cols].astype(F32)
        return rows, cols, u, v, x, go

    def local(d, g):
        cols = columns(g)
        for block in range(2):
            rows = pl.ds(block * STRETCH, STRETCH)
            scaled = wide[d, rows, cols].astype(F32) * dot(factor[d, rows], heads[:, cols])
            scaled = jnp.concatenate(split(scaled), axis=0)
            part[d, g, lax.rem(block + d, 2)] = dot(twice(masked[d, rows, narrow(g)], 0), scaled, TN)

    def intra(g):
        for block in range(2):
            rows, cols, u, v, x, go = views(g, block)
            b_in, c_in = b_v[rows, narrow(g)], c_v[rows, narrow(g)]
            gu, gu_low = split(go * u)
            xv, xv_low = split(x * v)
            scores, scores_low = split(dot(c_in, b_in, NT) * seen_s[rows])
            back, back_low = split(dot(b_in, c_in, NT) * seen_t[rows])
            y_s[rows, cols] = dot(scores, xv) + dot(scores, xv_low) + dot(scores_low, xv)
            z_s[rows, cols] = dot(back, gu) + dot(back, gu_low) + dot(back_low, gu)
            grad_scores = jnp.where(seen_s[rows] > 0.0, dot(gu, xv, NT), 0.0).astype(BF16)
            gc_s[rows, narrow(g)] = dot(grad_scores, b_in)
            gb_s[rows, narrow(g)] = dot(grad_scores, c_in, TN)
            skips = jnp.sum(x * go, axis=0, keepdims=True)
            skip_s[...] += by_head(jnp.broadcast_to(skips, (8, GROUP)), heads[:H, cols])
            if g == G - 1:
                from_z = x * v * z_s[rows, cols]
                net_s[rows] += by_head(go * u * y_s[rows, cols] - from_z, heads[:H, cols])
                late_s[rows] += by_head(from_z, heads[:H, cols])

    def weigh():
        g = G - 1
        cols = columns(g)
        for block in range(2):
            rows = pl.ds(block * STRETCH, STRETCH)
            x = wide[0, rows, cols].astype(F32)
            go = wide[1, rows, cols].astype(F32)
            cum, slope, dt = cum_s[rows], slope_s[rows], dt_s[rows]
            reach = rate * sum(dot(lows_half, part_slope) for part_slope in split(slope))
            u, k = jnp.exp(cum), jnp.exp(cum[STRETCH - 1 :] - cum) * dt
            plans = ((cum, -cum), (reach, slope / dt - reach))
            for kind, (on_states, on_later) in enumerate(plans):
                ahead = dot(jnp.concatenate(split(u * on_states), axis=1), heads[:, cols]) * go
                behind = dot(jnp.concatenate(split(k * on_later), axis=1), heads[:, cols]) * x
                ahead = jnp.concatenate(split(ahead), axis=0)
                behind = jnp.concatenate(split(behind), axis=0)
                at_end = jnp.broadcast_to(on_states[STRETCH - 1 :], (8, H))
                at_end = dot(jnp.concatenate(split(at_end), axis=1), heads[:, cols])
                weigh_s[kind, block, 0] = dot(twice(masked[1, rows, narrow(g)], 0), ahead, TN)
                weigh_s[kind, block, 1] = (
                    dot(twice(masked[0, rows, narrow(g)], 0), behind, TN) + at_end[:1] * part[0, g, block]
                )
                ahead_s[kind, block] = at_end * decay[block : block + 1, cols]

    def last_sums():
        lines = []
        for kind in range(2):
            line = jnp.zeros((1, GROUP), F32)
            for block in range(2):
                entering, later = state[0, G - 1, block], state[1, G - 1, 1 - block]
                line += jnp.sum(entering * weigh_s[kind, block, 0] + later * weigh_s[kind, block, 1], axis=0, keepdims=True)
                line += ahead_s[kind, block, :1] * jnp.sum(entering * later, axis=0, keepdims=True)
            lines.append(line)
        row = lax.broadcasted_iota(jnp.int32, (8, GROUP), 0)
        lines = jnp.where(row == 0, lines[0], jnp.where(row == 1, lines[1], 0.0))
        return by_head(lines, heads[:H, columns(G - 1)])

    def dt_gradients(block):
        rows = pl.ds(block * STRETCH, STRETCH)
        position = lax.broadcasted_iota(jnp.int32, (STRETCH, H), 0)
        grad_cum = net_s[rows] + jnp.where(position == STRETCH - 1, end_s[block * 8 : block * 8 + 1], 0.0)
        after = dot(triangle(False), grad_cum, precision=lax.Precision.HIGHEST)
        return grad_cum, (late_s[rows] / dt_s[rows] + rate * after) * slope_s[rows]

    def early_sums():
        sum_a = jnp.zeros((1, H), F32)
        sum_t = jnp.zeros((1, H), F32)
        for block in range(2):
            grad_cum, grad_dt = dt_gradients(block)
            sum_a += jnp.sum(cum_s[pl.ds(block * STRETCH, STRETCH)] * grad_cum, axis=0, keepdims=True)
            sum_t += jnp.sum(grad_dt, axis=0, keepdims=True)
        row = lax.broadcasted_iota(jnp.int32, (8, H), 0)
        early_s[...] = jnp.where(row == 0, sum_a, jnp.where(row == 1, sum_t, jnp.where(row == 2, skip_s[:1], 0.0)))

    def final_sums(g):
        for block in range(2):
            rows, cols, u, v, x, go = views(g, block)
            where = heads[:H, cols]
            entering, later = state[0, g, block], state[1, g, 1 - block]
            c_enter = twice(masked[1, rows, narrow(g)], 1)
            b_stay = twice(masked[0, rows, narrow(g)], 1)
            from_state = dot(c_enter, jnp.concatenate(split(entering), axis=0))
            y = y_s[rows, cols] + from_state
            from_later = u[STRETCH - 1 :] * dot(b_stay, jnp.concatenate(split(later), axis=0))
            z = z_s[rows, cols] + from_later
            y_s[rows, cols] = y
            z_s[rows, cols] = z
            xv = x * v
            if g == G - 1:
                y, z = from_state, from_later
            from_z = xv * z
            net_s[rows] += by_head(go * u * y - from_z, where)
            late_s[rows] += by_head(from_z, where)
            ends = jnp.sum(xv * from_later, axis=0, keepdims=True)
            ends += decay[block : block + 1, cols] * jnp.sum(entering * later, axis=0, keepdims=True)
            end_s[block * 8 : (block + 1) * 8] += by_head(jnp.broadcast_to(ends, (8, GROUP)), where)

    def final_out(g):
        skip = skip_row[:, g * GROUP : (g + 1) * GROUP]
        for block in range(2):
            rows, cols, u, v, x, go = views(g, block)
            mixed[rows, cols] = (u * y_s[rows, cols] + skip * x).astype(BF16)
            gx[rows, cols] = (v * z_s[rows, cols] + skip * go).astype(BF16)
            gu = (go * u).astype(BF16)
            xk = (x * (v * u[STRETCH - 1 :])).astype(BF16)
            entering, later = state[0, g, block].astype(BF16), state[1, g, 1 - block].astype(BF16)
            gc[rows, narrow(g)] = (gc_s[rows, narrow(g)] + enter_s[rows] * dot(gu, entering, NT)).astype(BF16)
            gb[rows, narrow(g)] = (gb_s[rows, narrow(g)] + stay_s[rows] * dot(xk, later, NT)).astype(BF16)

    at_zero = side == 0
    first = [at_zero, jnp.logical_not(at_zero)]

    def factors():
        mine = [jnp.where(at_zero, decay[s : s + 1], decay[1 - s : 2 - s]) for s in range(2)]
        theirs = [jnp.where(at_zero, z_decay[s : s + 1], z_decay[1 - s : 2 - s]) for s in range(2)]
        return mine, theirs

    def part_of(row, g):
        return row[:, g * GROUP : (g + 1) * GROUP]

    def combine(g):
        if g == 0:
            z_decays().wait_recv()
            z_decay[...] = expand(ends_there[...])
        z_up(g).wait_recv()
        mine, theirs = factors()
        if g == 0:
            pair = [mine[s] * theirs[s] for s in range(2)]
            for t in range(TILES):
                lines = [
                    pair[s][:, h * GROUP + t * LANES : h * GROUP + (t + 1) * LANES] for h in range(G) for s in range(2)
                ]
                lines = jnp.concatenate(lines, axis=0)
                for o in range(t, XY, TILES):
                    up[o, :8] = lines
        for s in range(2):
            scale_mine = jnp.where(first[s], part_of(theirs[s], g), 1.0)
            scale_theirs = jnp.where(first[s], 1.0, part_of(mine[s], g))
            total = scale_mine * part[side, g, s] + scale_theirs * z_in[g, s]
            for o in range(XY):
                band, t = o // TILES, o % TILES
                up[o, pl.ds(8 + (2 * g + s) * BAND, BAND)] = total[
                    band * BAND : (band + 1) * BAND, t * LANES : (t + 1) * LANES
                ]
        each_peer(lambda k: up_copy(g, k).start())
        up_in[place, up_rows(g)] = up[place, up_rows(g)]

    def scan(g):
        each_peer(lambda k: up_copy(g, k).wait_recv())

        def rise(j, now):
            down[j, pl.ds(2 * g * BAND, BAND)] = now
            return up_in[j, 2 * g : 2 * g + 1] * now + up_in[j, pl.ds(8 + 2 * g * BAND, BAND)]

        def fall(k, now):
            j = XY - 1 - k
            down[j, pl.ds((2 * g + 1) * BAND, BAND)] = now
            return up_in[j, 2 * g + 1 : 2 * g + 2] * now + up_in[j, pl.ds(8 + (2 * g + 1) * BAND, BAND)]

        now = lax.fori_loop(0, XY, rise, jnp.zeros((BAND, LANES), F32))
        lax.fori_loop(0, XY, fall, now)
        each_peer(lambda k: down_copy(g, k).start())
        down_in[place, down_rows(g)] = down[place, down_rows(g)]

    def spread(g):
        each_peer(lambda k: down_copy(g, k).wait_recv())
        mine, theirs = factors()
        for s in range(2):
            at = pl.ds((2 * g + s) * BAND, BAND)
            enter = jnp.concatenate(
                [
                    jnp.concatenate([down_in[r * TILES + t, at] for t in range(TILES)], axis=1)
                    for r in range(XY // TILES)
                ],
                axis=0,
            )
            keep = jnp.where(first[s], 1.0, part_of(theirs[s], g))
            keep_add = jnp.where(first[s], 0.0, 1.0)
            give = jnp.where(first[s], part_of(mine[s], g), 1.0)
            give_add = jnp.where(first[s], 1.0, 0.0)
            z_out[g, s] = give * enter + give_add * part[side, g, s]
            state[side, g, s] = keep * enter + keep_add * z_in[g, s]
        z_back(g).start()

    for copy in wide_in[0]:
        copy.wait()
    local(1 - side, 0)
    pl.semaphore_wait(barrier, XY + FAR - 2)
    z_decays().start()
    z_up(0).start()
    prepare()
    skip_row = expand(jnp.broadcast_to(sk[...], (8, H)))[:1]
    for g in range(1, G):
        for copy in wide_in[g]:
            copy.wait()
        local(1 - side, g)
        z_up(g).start()
    for g in range(G):
        local(side, g)
    for g in range(G):
        intra(g)
        combine(g)
        if g >= 1:
            scan(g - 1)
        if g >= 2:
            spread(g - 2)
    scan(G - 1)
    spread(G - 2)
    z_back(0).wait_recv()
    final_sums(0)
    spread(G - 1)
    final_out(0)
    for g in range(G):
        z_up(g).wait_send()
        each_peer(lambda k: up_copy(g, k).wait_send())
        each_peer(lambda k: down_copy(g, k).wait_send())
    z_decays().wait_send()
    weigh()
    for g in range(1, G - 1):
        z_back(g).wait_recv()
        final_sums(g)
        final_out(g)
    early_sums()
    for g in range(G):
        z_back(g).wait_send()
    z_back(G - 1).wait_recv()
    params[...] = early_s[...] + last_sums()

    def sum1(k):
        return remote(params, buf1.at[k], s1.at[k], r1.at[k], near(k))

    def sum2(k):
        return remote(buf2.at[0], buf2.at[k], s2.at[k], r2.at[k], far(k))

    def each_far(act):
        def body(k, carry):
            act(k)
            return carry

        lax.fori_loop(1, FAR, body, 0)

    each_peer(lambda k: sum1(k).start())
    buf1[0] = params[...]
    final_sums(G - 1)
    final_out(G - 1)
    for block in range(2):
        gdt[:, block * STRETCH : (block + 1) * STRETCH] = jnp.transpose(dt_gradients(block)[1])
    each_peer(lambda k: sum1(k).wait_recv())
    buf2[0] = jnp.sum(buf1[...], axis=0)
    each_far(lambda k: sum2(k).start())
    each_peer(lambda k: sum1(k).wait_send())
    each_far(lambda k: sum2(k).wait_recv())
    total = jnp.zeros((8, H), F32)
    for g in range(FAR):
        total += buf2[lax.rem(g - mine_far + FAR, FAR)]
    grad_a[...] = total[0:1]
    grad_t[...] = total[1:2]
    grad_k[...] = total[2:3]
    each_far(lambda k: sum2(k).wait_send())


def store_kernel(*refs):
    count = len(refs) // 2
    sems = refs[-1]
    copies = []
    for src, dst in zip(refs[:count], refs[count:]):
        pieces = PIECES if src.shape[0] == ROWS else 1
        for i in range(pieces):
            rows = pl.ds(i * (src.shape[0] // pieces), src.shape[0] // pieces)
            copy = pltpu.make_async_copy(src.at[rows], dst.at[rows], sems.at[len(copies)])
            copy.start()
            copies.append(copy)
    for copy in copies:
        copy.wait()


def shards(hidden_x, b_proj, c_proj, dt_raw, span_start, a_log, skip_gain, dt_bias, out_grad):
    arrays = (
        hidden_x.reshape(ROWS, WIDTH),
        out_grad.reshape(ROWS, WIDTH),
        b_proj.reshape(ROWS, G * N),
        c_proj.reshape(ROWS, G * N),
        dt_raw.reshape(ROWS, H).T,
        span_start.reshape(1, ROWS),
        a_log.reshape(1, H),
        skip_gain.reshape(1, H),
        dt_bias.reshape(1, H),
    )
    anywhere = pl.BlockSpec(memory_space=pltpu.HBM)
    vmem = pl.BlockSpec(memory_space=pltpu.VMEM)
    dma = pltpu.SemaphoreType.DMA

    def f32(*shape):
        return pltpu.VMEM(shape, F32)

    def bf16(*shape):
        return pltpu.VMEM(shape, BF16)

    wide = jax.ShapeDtypeStruct((ROWS, WIDTH), BF16)
    slim = jax.ShapeDtypeStruct((ROWS, G * N), BF16)
    line = jax.ShapeDtypeStruct((1, H), F32)
    outs = (wide, wide, slim, slim, jax.ShapeDtypeStruct((H, ROWS), F32), line, line, line)
    held = tuple(pltpu.VMEM(out.shape, out.dtype) for out in outs)
    arrays = [pltpu.with_memory_space_constraint(a, pltpu.HBM) for a in arrays]
    results = pl.pallas_call(
        layer_kernel,
        out_shape=held,
        in_specs=[anywhere] * len(arrays),
        out_specs=(vmem,) * len(outs),
        scratch_shapes=[
            bf16(2, ROWS, WIDTH), bf16(ROWS, G * N), bf16(ROWS, G * N), f32(H, ROWS),
            pltpu.VMEM((1, ROWS), jnp.int32), f32(1, H), f32(1, H), f32(1, H),
            bf16(2 * H, WIDTH), f32(ROWS, H), f32(ROWS, H), f32(ROWS, H), bf16(2, ROWS, 2 * H), bf16(ROWS, 2 * H),
            bf16(2, ROWS, G * N), f32(ROWS, N), f32(ROWS, N), f32(ROWS, STRETCH), f32(ROWS, STRETCH),
            f32(ROWS, WIDTH), f32(ROWS, WIDTH),
            f32(ROWS, G * N), f32(ROWS, G * N), f32(ROWS, H), f32(ROWS, H), f32(16, H), f32(8, H),
            f32(2, 2, 2, N, GROUP), f32(2, 2, 8, GROUP), f32(8, H),
            f32(8, H), f32(8, H), f32(8, WIDTH), f32(8, WIDTH),
            f32(2, G, 2, N, GROUP), f32(2, G, 2, N, GROUP), f32(G, 2, N, GROUP), f32(G, 2, N, GROUP),
            f32(XY, 8 + 2 * N, LANES), f32(XY, 8 + 2 * N, LANES), f32(XY, 2 * N, LANES), f32(XY, 2 * N, LANES),
            f32(8, H), f32(XY, 8, H), f32(FAR, 8, H),
            dma((7 + 2 * G,)), dma((G + 1,)), dma((G + 1,)),
            dma((G, XY)), dma((G, XY)), dma((G, XY)), dma((G, XY)), dma((G,)), dma((G,)),
            dma((XY,)), dma((XY,)), dma((FAR,)), dma((FAR,)),
        ],
        compiler_params=pltpu.CompilerParams(
            collective_id=0, has_side_effects=True, vmem_limit_bytes=44 * 2**20
        ),
        cost_estimate=pl.CostEstimate(flops=5 * 10**9, bytes_accessed=10 * 2**20, transcendentals=10**5),
        name="layer",
    )(*arrays)
    mixed, gx, gb, gc, gdt, grad_a, grad_k, grad_t = pl.pallas_call(
        store_kernel,
        out_shape=outs,
        in_specs=[vmem] * len(outs),
        out_specs=(anywhere,) * len(outs),
        scratch_shapes=[dma((4 * PIECES + 4,))],
        compiler_params=pltpu.CompilerParams(vmem_limit_bytes=2**20),
        name="store",
    )(*[pltpu.with_memory_space_constraint(r, pltpu.VMEM) for r in results])
    return (
        mixed.reshape(1, ROWS, WIDTH),
        gx.reshape(1, ROWS, WIDTH),
        gb.reshape(1, ROWS, G * N),
        gc.reshape(1, ROWS, G * N),
        gdt.T.reshape(1, ROWS, H),
        grad_a.reshape(H),
        grad_k.reshape(H),
        grad_t.reshape(H),
    )


def solution(mesh):
    rows = P("dp", "ctx", None)
    return jax.shard_map(
        shards,
        mesh=mesh,
        in_specs=(rows, rows, rows, rows, P("dp", "ctx"), P(), P(), P(), rows),
        out_specs=(rows, rows, rows, rows, rows, P(), P(), P()),
        check_vma=False,
    )
```

```python
import jax
import jax.numpy as jnp
from jax import lax
from jax.experimental import pallas as pl
from jax.experimental.pallas import tpu as pltpu
from jax.sharding import PartitionSpec as P

H = 64
P_SIZE = 32
N = 64
G = 4
STRETCH = 256
ROWS = 2 * STRETCH
WIDTH = H * P_SIZE
GROUP = WIDTH // G
XY = 16
LANES = 128
TILES = GROUP // LANES
BAND = N // (XY // TILES)
FAR = 8
PIECES = 4
F32 = jnp.float32
BF16 = jnp.bfloat16
MESH = pl.DeviceIdType.MESH
NN = ((1,), (0,))
NT = ((1,), (1,))
TN = ((0,), (0,))


def dot(a, b, dims=NN, precision=None):
    return lax.dot_general(a, b, (dims, ((), ())), preferred_element_type=F32, precision=precision)


def split(a):
    high = a.astype(BF16)
    return high, (a - high.astype(F32)).astype(BF16)


def triangle(lower):
    row = lax.broadcasted_iota(jnp.int32, (STRETCH, STRETCH), 0)
    column = lax.broadcasted_iota(jnp.int32, (STRETCH, STRETCH), 1)
    return jnp.where(row >= column if lower else row <= column, 1.0, 0.0)


def layer_kernel(
    x_hbm, go_hbm, b_hbm, c_hbm, dt_hbm, start_hbm, al_hbm, sk_hbm, tb_hbm,
    mixed, gx, gb, gc, gdt, grad_a, grad_k, grad_t,
    wide, b_v, c_v, dt_v, start_v, al, sk, tb,
    heads, dt_s, slope_s, cum_s, factor, v_s, masked, enter_s, stay_s, seen_s, seen_t,
    y_s, z_s, gb_s, gc_s, net_s, late_s, end_s, skip_s, weigh_s, ahead_s, early_s,
    ends_here, ends_there, decay, z_decay, part, state, z_in, z_out, up, up_in, down, down_in, params, buf1, buf2,
    in_sem, z_s_sem, z_r_sem, up_s_sem, up_r_sem, down_s_sem, down_r_sem, back_s_sem, back_r_sem,
    s1, r1, s2, r2,
):
    here, dp = lax.axis_index("ctx"), lax.axis_index("dp")
    side, place = lax.rem(here, 2), here // 2
    partner = {"ctx": here + 1 - 2 * side}
    mine_far = dp * 2 + side

    def peer(k):
        return lax.rem(place + k, XY)

    def near(k):
        return {"ctx": peer(k) * 2 + side}

    def far(k):
        g = lax.rem(mine_far + k, FAR)
        return {"dp": g // 2, "ctx": place * 2 + lax.rem(g, 2)}

    loads = []

    def load(src, dst):
        copy = pltpu.make_async_copy(src, dst, in_sem.at[len(loads)])
        copy.start()
        loads.append(copy)
        return copy

    def columns(g):
        return pl.ds(g * GROUP, GROUP)

    def load_wide(d, g):
        return load((x_hbm, go_hbm)[d].at[:, columns(g)], wide.at[d, :, columns(g)])

    small = [load(s, d) for s, d in ((dt_hbm, dt_v), (start_hbm, start_v), (al_hbm, al), (tb_hbm, tb), (sk_hbm, sk))]
    small += [load(b_hbm, b_v), load(c_hbm, c_v)]
    wide_in = [[load_wide(0, 0), load_wide(1, 0)]]

    barrier = pltpu.get_barrier_semaphore()

    def greet_near(k, carry):
        pl.semaphore_signal(barrier, inc=1, device_id=near(k), device_id_type=MESH)
        return carry

    def greet_far(k, carry):
        pl.semaphore_signal(barrier, inc=1, device_id=far(k), device_id_type=MESH)
        return carry

    lax.fori_loop(1, XY, greet_near, 0)
    lax.fori_loop(1, FAR, greet_far, 0)

    def remote(src, dst, send, recv, to):
        return pltpu.make_async_remote_copy(
            src_ref=src, dst_ref=dst, send_sem=send, recv_sem=recv, device_id=to, device_id_type=MESH
        )

    def z_up(g):
        return remote(part.at[1 - side, g], z_in.at[g], z_s_sem.at[0], z_r_sem.at[g], partner)

    def z_decays():
        return remote(ends_here, ends_there, z_s_sem.at[1], z_r_sem.at[G], partner)

    def up_rows(g):
        return pl.ds(8 + g * 2 * BAND, 2 * BAND) if g else pl.ds(0, 8 + 2 * BAND)

    def up_copy(g, k):
        return remote(up.at[peer(k), up_rows(g)], up_in.at[place, up_rows(g)], up_s_sem.at[0], up_r_sem.at[g], near(k))

    def down_rows(g):
        return pl.ds(g * 2 * BAND, 2 * BAND)

    def down_copy(g, k):
        return remote(down.at[peer(k), down_rows(g)], down_in.at[place, down_rows(g)], down_s_sem.at[0], down_r_sem.at[g], near(k))

    def z_back(g):
        return remote(z_out.at[g], state.at[side, g], back_s_sem.at[0], back_r_sem.at[g], partner)

    def received(ref, sem):
        remote(ref, ref, z_s_sem.at[0], sem, partner).wait_recv()

    def sent(ref, sem):
        remote(ref, ref, sem, z_r_sem.at[0], partner).wait_send()

    others = pl.ds(0, XY - 1)

    def each_peer(act):
        def body(k, carry):
            act(k)
            return carry

        lax.fori_loop(1, XY, body, 0)

    def map_heads(g):
        head = lax.broadcasted_iota(jnp.int32, (H, GROUP), 0)
        column = lax.broadcasted_iota(jnp.int32, (H, GROUP), 1) + g * GROUP
        mapped = jnp.where(column // P_SIZE == head, 1.0, 0.0).astype(BF16)
        heads[:H, columns(g)] = mapped
        heads[H:, columns(g)] = mapped

    def expand(values):
        return dot(jnp.concatenate(split(values), axis=1), heads[...])

    map_heads(0)
    lows = triangle(True)
    lows_half = lows.astype(BF16)
    for copy in small:
        copy.wait()
    for g in range(1, G):
        wide_in.append([load_wide(0, g), load_wide(1, g)])
    rate = -jnp.exp(al[...])
    lasts, spans = [], []
    for block in range(2):
        rows = pl.ds(block * STRETCH, STRETCH)
        shifted = jnp.transpose(dt_v[:, block * STRETCH : (block + 1) * STRETCH]) + tb[...]
        tail = jnp.exp(-jnp.abs(shifted))
        dt = jnp.maximum(shifted, 0.0) + jnp.log1p(tail)
        dt_s[rows] = dt
        slope_s[rows] = jnp.where(shifted >= 0.0, 1.0, tail) / (1.0 + tail)
        dt_high, dt_rest = split(dt)
        dt_low = (dt - dt_high.astype(F32) - dt_rest.astype(F32)).astype(BF16)
        cum = rate * (dot(lows_half, dt_high) + dot(lows_half, dt_rest) + dot(lows_half, dt_low))
        cum_s[rows] = cum
        last = cum[STRETCH - 1 :]
        factor[0, rows] = jnp.concatenate(split(jnp.exp(last - cum) * dt), axis=1)
        factor[1, rows] = jnp.concatenate(split(jnp.exp(cum)), axis=1)
        v_s[rows] = jnp.concatenate(split(jnp.exp(-cum) * dt), axis=1)
        start = jnp.broadcast_to(start_v[:, block * STRETCH : (block + 1) * STRETCH].astype(F32), (8, STRETCH))
        start = start.astype(BF16)
        count = dot(lows_half, start, NT)[:, :1]
        spans.append((count, start))
        enters = jnp.where(count == 0.0, 1.0, 0.0)
        stays = jnp.where(count == count[STRETCH - 1 :], 1.0, 0.0)
        masked[0, rows] = (b_v[rows].astype(F32) * stays).astype(BF16)
        masked[1, rows] = (c_v[rows].astype(F32) * enters).astype(BF16)
        enter_s[rows] = jnp.broadcast_to(enters, (STRETCH, N))
        stay_s[rows] = jnp.broadcast_to(stays, (STRETCH, N))
        lasts.append(jnp.exp(last) * jnp.where(count[STRETCH - 1 :] == 0.0, 1.0, 0.0))
    row = lax.broadcasted_iota(jnp.int32, (8, H), 0)
    ends_here[...] = jnp.where(row == 0, lasts[0], jnp.where(row == 1, lasts[1], 0.0))

    def prepare():
        for g in range(1, G):
            map_heads(g)
        for block in range(2):
            rows = pl.ds(block * STRETCH, STRETCH)
            count, start = spans[block]
            same = jnp.where(count == dot(start, lows_half, NT)[:1], 1.0, 0.0)
            seen_s[rows] = same * lows
            seen_t[rows] = same * triangle(False)
        decay[...] = expand(ends_here[...])
        net_s[...] = jnp.zeros_like(net_s)
        late_s[...] = jnp.zeros_like(late_s)
        end_s[...] = jnp.zeros_like(end_s)
        skip_s[...] = jnp.zeros_like(skip_s)

    def narrow(g):
        return slice(g * N, (g + 1) * N)

    def by_head(values, where):
        high, low = split(values)
        return dot(high, where, NT) + dot(low, where, NT)

    def twice(a, axis):
        return jnp.concatenate([a, a], axis=axis)

    def views(g, block):
        rows, cols = pl.ds(block * STRETCH, STRETCH), columns(g)
        u = dot(factor[1, rows], heads[:, cols])
        v = dot(v_s[rows], heads[:, cols])
        x = wide[0, rows, cols].astype(F32)
        go = wide[1, rows, cols].astype(F32)
        return rows, cols, u, v, x, go

    def local(d, g):
        cols = columns(g)
        for block in range(2):
            rows = pl.ds(block * STRETCH, STRETCH)
            scaled = wide[d, rows, cols].astype(F32) * dot(factor[d, rows], heads[:, cols])
            scaled = jnp.concatenate(split(scaled), axis=0)
            part[d, g, lax.rem(block + d, 2)] = dot(twice(masked[d, rows, narrow(g)], 0), scaled, TN)

    def intra(g):
        for block in range(2):
            rows, cols, u, v, x, go = views(g, block)
            b_in, c_in = b_v[rows, narrow(g)], c_v[rows, narrow(g)]
            gu, gu_low = split(go * u)
            xv, xv_low = split(x * v)
            scores, scores_low = split(dot(c_in, b_in, NT) * seen_s[rows])
            back, back_low = split(dot(b_in, c_in, NT) * seen_t[rows])
            y_s[rows, cols] = dot(scores, xv) + dot(scores, xv_low) + dot(scores_low, xv)
            z_s[rows, cols] = dot(back, gu) + dot(back, gu_low) + dot(back_low, gu)
            grad_scores = jnp.where(seen_s[rows] > 0.0, dot(gu, xv, NT), 0.0).astype(BF16)
            gc_s[rows, narrow(g)] = dot(grad_scores, b_in)
            gb_s[rows, narrow(g)] = dot(grad_scores, c_in, TN)
            skips = jnp.sum(x * go, axis=0, keepdims=True)
            skip_s[...] += by_head(jnp.broadcast_to(skips, (8, GROUP)), heads[:H, cols])
            if g == G - 1:
                from_z = x * v * z_s[rows, cols]
                net_s[rows] += by_head(go * u * y_s[rows, cols] - from_z, heads[:H, cols])
                late_s[rows] += by_head(from_z, heads[:H, cols])

    def weigh():
        g = G - 1
        cols = columns(g)
        for block in range(2):
            rows = pl.ds(block * STRETCH, STRETCH)
            x = wide[0, rows, cols].astype(F32)
            go = wide[1, rows, cols].astype(F32)
            cum, slope, dt = cum_s[rows], slope_s[rows], dt_s[rows]
            reach = rate * sum(dot(lows_half, part_slope) for part_slope in split(slope))
            u, k = jnp.exp(cum), jnp.exp(cum[STRETCH - 1 :] - cum) * dt
            plans = ((cum, -cum), (reach, slope / dt - reach))
            for kind, (on_states, on_later) in enumerate(plans):
                ahead = dot(jnp.concatenate(split(u * on_states), axis=1), heads[:, cols]) * go
                behind = dot(jnp.concatenate(split(k * on_later), axis=1), heads[:, cols]) * x
                ahead = jnp.concatenate(split(ahead), axis=0)
                behind = jnp.concatenate(split(behind), axis=0)
                at_end = jnp.broadcast_to(on_states[STRETCH - 1 :], (8, H))
                at_end = dot(jnp.concatenate(split(at_end), axis=1), heads[:, cols])
                weigh_s[kind, block, 0] = dot(twice(masked[1, rows, narrow(g)], 0), ahead, TN)
                weigh_s[kind, block, 1] = (
                    dot(twice(masked[0, rows, narrow(g)], 0), behind, TN) + at_end[:1] * part[0, g, block]
                )
                ahead_s[kind, block] = at_end * decay[block : block + 1, cols]

    def last_sums():
        lines = []
        for kind in range(2):
            line = jnp.zeros((1, GROUP), F32)
            for block in range(2):
                entering, later = state[0, G - 1, block], state[1, G - 1, 1 - block]
                line += jnp.sum(entering * weigh_s[kind, block, 0] + later * weigh_s[kind, block, 1], axis=0, keepdims=True)
                line += ahead_s[kind, block, :1] * jnp.sum(entering * later, axis=0, keepdims=True)
            lines.append(line)
        row = lax.broadcasted_iota(jnp.int32, (8, GROUP), 0)
        lines = jnp.where(row == 0, lines[0], jnp.where(row == 1, lines[1], 0.0))
        return by_head(lines, heads[:H, columns(G - 1)])

    def dt_gradients(block):
        rows = pl.ds(block * STRETCH, STRETCH)
        position = lax.broadcasted_iota(jnp.int32, (STRETCH, H), 0)
        grad_cum = net_s[rows] + jnp.where(position == STRETCH - 1, end_s[block * 8 : block * 8 + 1], 0.0)
        after = dot(triangle(False), grad_cum, precision=lax.Precision.HIGHEST)
        return grad_cum, (late_s[rows] / dt_s[rows] + rate * after) * slope_s[rows]

    def early_sums():
        sum_a = jnp.zeros((1, H), F32)
        sum_t = jnp.zeros((1, H), F32)
        for block in range(2):
            grad_cum, grad_dt = dt_gradients(block)
            sum_a += jnp.sum(cum_s[pl.ds(block * STRETCH, STRETCH)] * grad_cum, axis=0, keepdims=True)
            sum_t += jnp.sum(grad_dt, axis=0, keepdims=True)
        row = lax.broadcasted_iota(jnp.int32, (8, H), 0)
        early_s[...] = jnp.where(row == 0, sum_a, jnp.where(row == 1, sum_t, jnp.where(row == 2, skip_s[:1], 0.0)))

    def final_sums(g):
        for block in range(2):
            rows, cols, u, v, x, go = views(g, block)
            where = heads[:H, cols]
            entering, later = state[0, g, block], state[1, g, 1 - block]
            c_enter = twice(masked[1, rows, narrow(g)], 1)
            b_stay = twice(masked[0, rows, narrow(g)], 1)
            from_state = dot(c_enter, jnp.concatenate(split(entering), axis=0))
            y = y_s[rows, cols] + from_state
            from_later = u[STRETCH - 1 :] * dot(b_stay, jnp.concatenate(split(later), axis=0))
            z = z_s[rows, cols] + from_later
            y_s[rows, cols] = y
            z_s[rows, cols] = z
            xv = x * v
            if g == G - 1:
                y, z = from_state, from_later
            from_z = xv * z
            net_s[rows] += by_head(go * u * y - from_z, where)
            late_s[rows] += by_head(from_z, where)
            ends = jnp.sum(xv * from_later, axis=0, keepdims=True)
            ends += decay[block : block + 1, cols] * jnp.sum(entering * later, axis=0, keepdims=True)
            end_s[block * 8 : (block + 1) * 8] += by_head(jnp.broadcast_to(ends, (8, GROUP)), where)

    def final_out(g):
        skip = skip_row[:, g * GROUP : (g + 1) * GROUP]
        for block in range(2):
            rows, cols, u, v, x, go = views(g, block)
            mixed[rows, cols] = (u * y_s[rows, cols] + skip * x).astype(BF16)
            gx[rows, cols] = (v * z_s[rows, cols] + skip * go).astype(BF16)
            gu = (go * u).astype(BF16)
            xk = (x * (v * u[STRETCH - 1 :])).astype(BF16)
            entering, later = state[0, g, block].astype(BF16), state[1, g, 1 - block].astype(BF16)
            gc[rows, narrow(g)] = (gc_s[rows, narrow(g)] + enter_s[rows] * dot(gu, entering, NT)).astype(BF16)
            gb[rows, narrow(g)] = (gb_s[rows, narrow(g)] + stay_s[rows] * dot(xk, later, NT)).astype(BF16)

    at_zero = side == 0
    first = [at_zero, jnp.logical_not(at_zero)]

    def factors():
        mine = [jnp.where(at_zero, decay[s : s + 1], decay[1 - s : 2 - s]) for s in range(2)]
        theirs = [jnp.where(at_zero, z_decay[s : s + 1], z_decay[1 - s : 2 - s]) for s in range(2)]
        return mine, theirs

    def part_of(row, g):
        return row[:, g * GROUP : (g + 1) * GROUP]

    def combine(g):
        if g == 0:
            z_decays().wait_recv()
            z_decay[...] = expand(ends_there[...])
        z_up(g).wait_recv()
        mine, theirs = factors()
        if g == 0:
            pair = [mine[s] * theirs[s] for s in range(2)]
            for t in range(TILES):
                lines = [
                    pair[s][:, h * GROUP + t * LANES : h * GROUP + (t + 1) * LANES] for h in range(G) for s in range(2)
                ]
                lines = jnp.concatenate(lines, axis=0)
                for o in range(t, XY, TILES):
                    up[o, :8] = lines
        for s in range(2):
            scale_mine = jnp.where(first[s], part_of(theirs[s], g), 1.0)
            scale_theirs = jnp.where(first[s], 1.0, part_of(mine[s], g))
            total = scale_mine * part[side, g, s] + scale_theirs * z_in[g, s]
            for o in range(XY):
                band, t = o // TILES, o % TILES
                up[o, pl.ds(8 + (2 * g + s) * BAND, BAND)] = total[
                    band * BAND : (band + 1) * BAND, t * LANES : (t + 1) * LANES
                ]
        each_peer(lambda k: up_copy(g, k).start())
        up_in[place, up_rows(g)] = up[place, up_rows(g)]

    def scan(g):
        received(up_in.at[others, up_rows(g)], up_r_sem.at[g])

        def rise(j, now):
            down[j, pl.ds(2 * g * BAND, BAND)] = now
            return up_in[j, 2 * g : 2 * g + 1] * now + up_in[j, pl.ds(8 + 2 * g * BAND, BAND)]

        def fall(k, now):
            j = XY - 1 - k
            down[j, pl.ds((2 * g + 1) * BAND, BAND)] = now
            return up_in[j, 2 * g + 1 : 2 * g + 2] * now + up_in[j, pl.ds(8 + (2 * g + 1) * BAND, BAND)]

        now = lax.fori_loop(0, XY, rise, jnp.zeros((BAND, LANES), F32))
        lax.fori_loop(0, XY, fall, now)
        each_peer(lambda k: down_copy(g, k).start())
        down_in[place, down_rows(g)] = down[place, down_rows(g)]

    def spread(g):
        received(down_in.at[others, down_rows(g)], down_r_sem.at[g])
        mine, theirs = factors()
        for s in range(2):
            at = pl.ds((2 * g + s) * BAND, BAND)
            enter = jnp.concatenate(
                [
                    jnp.concatenate([down_in[r * TILES + t, at] for t in range(TILES)], axis=1)
                    for r in range(XY // TILES)
                ],
                axis=0,
            )
            keep = jnp.where(first[s], 1.0, part_of(theirs[s], g))
            keep_add = jnp.where(first[s], 0.0, 1.0)
            give = jnp.where(first[s], part_of(mine[s], g), 1.0)
            give_add = jnp.where(first[s], 1.0, 0.0)
            z_out[g, s] = give * enter + give_add * part[side, g, s]
            state[side, g, s] = keep * enter + keep_add * z_in[g, s]
        z_back(g).start()

    for copy in wide_in[0]:
        copy.wait()
    local(1 - side, 0)
    pl.semaphore_wait(barrier, XY + FAR - 2)
    z_decays().start()
    z_up(0).start()
    prepare()
    skip_row = expand(jnp.broadcast_to(sk[...], (8, H)))[:1]
    for g in range(1, G):
        for copy in wide_in[g]:
            copy.wait()
        local(1 - side, g)
        z_up(g).start()
    for g in range(G):
        local(side, g)
    for g in range(G):
        intra(g)
        combine(g)
        if g >= 1:
            scan(g - 1)
        if g >= 2:
            spread(g - 2)
    scan(G - 1)
    spread(G - 2)
    z_back(0).wait_recv()
    final_sums(0)
    spread(G - 1)
    final_out(0)
    z_decays().wait_send()
    sent(z_in, z_s_sem.at[0])
    sent(up.at[others], up_s_sem.at[0])
    sent(down.at[others], down_s_sem.at[0])
    weigh()
    for g in range(1, G - 1):
        z_back(g).wait_recv()
        final_sums(g)
        final_out(g)
    early_sums()
    sent(z_out, back_s_sem.at[0])
    z_back(G - 1).wait_recv()
    params[...] = early_s[...] + last_sums()

    def sum1(k):
        return remote(params, buf1.at[k], s1.at[0], r1.at[0], near(k))

    def sum2(k):
        return remote(buf2.at[0], buf2.at[k], s2.at[0], r2.at[0], far(k))

    def each_far(act):
        def body(k, carry):
            act(k)
            return carry

        lax.fori_loop(1, FAR, body, 0)

    each_peer(lambda k: sum1(k).start())
    buf1[0] = params[...]
    final_sums(G - 1)
    final_out(G - 1)
    for block in range(2):
        gdt[:, block * STRETCH : (block + 1) * STRETCH] = jnp.transpose(dt_gradients(block)[1])
    received(buf1.at[pl.ds(1, XY - 1)], r1.at[0])
    buf2[0] = jnp.sum(buf1[...], axis=0)
    each_far(lambda k: sum2(k).start())
    sent(buf1.at[pl.ds(1, XY - 1)], s1.at[0])
    received(buf2.at[pl.ds(1, FAR - 1)], r2.at[0])
    total = jnp.zeros((8, H), F32)
    for g in range(FAR):
        total += buf2[lax.rem(g - mine_far + FAR, FAR)]
    grad_a[...] = total[0:1]
    grad_t[...] = total[1:2]
    grad_k[...] = total[2:3]
    sent(buf2.at[pl.ds(1, FAR - 1)], s2.at[0])


def store_kernel(*refs):
    count = len(refs) // 2
    sems = refs[-1]
    copies = []
    for src, dst in zip(refs[:count], refs[count:]):
        pieces = PIECES if src.shape[0] == ROWS else 1
        for i in range(pieces):
            rows = pl.ds(i * (src.shape[0] // pieces), src.shape[0] // pieces)
            copy = pltpu.make_async_copy(src.at[rows], dst.at[rows], sems.at[len(copies)])
            copy.start()
            copies.append(copy)
    for copy in copies:
        copy.wait()


def shards(hidden_x, b_proj, c_proj, dt_raw, span_start, a_log, skip_gain, dt_bias, out_grad):
    arrays = (
        hidden_x.reshape(ROWS, WIDTH),
        out_grad.reshape(ROWS, WIDTH),
        b_proj.reshape(ROWS, G * N),
        c_proj.reshape(ROWS, G * N),
        dt_raw.reshape(ROWS, H).T,
        span_start.reshape(1, ROWS),
        a_log.reshape(1, H),
        skip_gain.reshape(1, H),
        dt_bias.reshape(1, H),
    )
    anywhere = pl.BlockSpec(memory_space=pltpu.HBM)
    vmem = pl.BlockSpec(memory_space=pltpu.VMEM)
    dma = pltpu.SemaphoreType.DMA

    def f32(*shape):
        return pltpu.VMEM(shape, F32)

    def bf16(*shape):
        return pltpu.VMEM(shape, BF16)

    wide = jax.ShapeDtypeStruct((ROWS, WIDTH), BF16)
    slim = jax.ShapeDtypeStruct((ROWS, G * N), BF16)
    line = jax.ShapeDtypeStruct((1, H), F32)
    outs = (wide, wide, slim, slim, jax.ShapeDtypeStruct((H, ROWS), F32), line, line, line)
    held = tuple(pltpu.VMEM(out.shape, out.dtype) for out in outs)
    arrays = [pltpu.with_memory_space_constraint(a, pltpu.HBM) for a in arrays]
    results = pl.pallas_call(
        layer_kernel,
        out_shape=held,
        in_specs=[anywhere] * len(arrays),
        out_specs=(vmem,) * len(outs),
        scratch_shapes=[
            bf16(2, ROWS, WIDTH), bf16(ROWS, G * N), bf16(ROWS, G * N), f32(H, ROWS),
            pltpu.VMEM((1, ROWS), jnp.int32), f32(1, H), f32(1, H), f32(1, H),
            bf16(2 * H, WIDTH), f32(ROWS, H), f32(ROWS, H), f32(ROWS, H), bf16(2, ROWS, 2 * H), bf16(ROWS, 2 * H),
            bf16(2, ROWS, G * N), f32(ROWS, N), f32(ROWS, N), f32(ROWS, STRETCH), f32(ROWS, STRETCH),
            f32(ROWS, WIDTH), f32(ROWS, WIDTH),
            f32(ROWS, G * N), f32(ROWS, G * N), f32(ROWS, H), f32(ROWS, H), f32(16, H), f32(8, H),
            f32(2, 2, 2, N, GROUP), f32(2, 2, 8, GROUP), f32(8, H),
            f32(8, H), f32(8, H), f32(8, WIDTH), f32(8, WIDTH),
            f32(2, G, 2, N, GROUP), f32(2, G, 2, N, GROUP), f32(G, 2, N, GROUP), f32(G, 2, N, GROUP),
            f32(XY, 8 + 2 * N, LANES), f32(XY, 8 + 2 * N, LANES), f32(XY, 2 * N, LANES), f32(XY, 2 * N, LANES),
            f32(8, H), f32(XY, 8, H), f32(FAR, 8, H),
            dma((7 + 2 * G,)), dma((2,)), dma((G + 1,)),
            dma((1,)), dma((G,)), dma((1,)), dma((G,)), dma((1,)), dma((G,)),
            dma((1,)), dma((1,)), dma((1,)), dma((1,)),
        ],
        compiler_params=pltpu.CompilerParams(
            collective_id=0, has_side_effects=True, vmem_limit_bytes=44 * 2**20
        ),
        cost_estimate=pl.CostEstimate(flops=5 * 10**9, bytes_accessed=10 * 2**20, transcendentals=10**5),
        name="layer",
    )(*arrays)
    mixed, gx, gb, gc, gdt, grad_a, grad_k, grad_t = pl.pallas_call(
        store_kernel,
        out_shape=outs,
        in_specs=[vmem] * len(outs),
        out_specs=(anywhere,) * len(outs),
        scratch_shapes=[dma((4 * PIECES + 4,))],
        compiler_params=pltpu.CompilerParams(vmem_limit_bytes=2**20),
        name="store",
    )(*[pltpu.with_memory_space_constraint(r, pltpu.VMEM) for r in results])
    return (
        mixed.reshape(1, ROWS, WIDTH),
        gx.reshape(1, ROWS, WIDTH),
        gb.reshape(1, ROWS, G * N),
        gc.reshape(1, ROWS, G * N),
        gdt.T.reshape(1, ROWS, H),
        grad_a.reshape(H),
        grad_k.reshape(H),
        grad_t.reshape(H),
    )


def solution(mesh):
    rows = P("dp", "ctx", None)
    return jax.shard_map(
        shards,
        mesh=mesh,
        in_specs=(rows, rows, rows, rows, P("dp", "ctx"), P(), P(), P(), rows),
        out_specs=(rows, rows, rows, rows, rows, P(), P(), P()),
        check_vma=False,
    )
```

```python
import jax
import jax.numpy as jnp
from jax import lax
from jax.experimental import pallas as pl
from jax.experimental.pallas import tpu as pltpu
from jax.sharding import PartitionSpec as P

H = 64
P_SIZE = 32
N = 64
G = 4
STRETCH = 256
ROWS = 2 * STRETCH
WIDTH = H * P_SIZE
GROUP = WIDTH // G
XY = 16
LANES = 128
TILES = GROUP // LANES
BAND = N // (XY // TILES)
FAR = 8
PIECES = 4
F32 = jnp.float32
BF16 = jnp.bfloat16
MESH = pl.DeviceIdType.MESH
NN = ((1,), (0,))
NT = ((1,), (1,))
TN = ((0,), (0,))


def dot(a, b, dims=NN, precision=None):
    return lax.dot_general(a, b, (dims, ((), ())), preferred_element_type=F32, precision=precision)


def split(a):
    high = a.astype(BF16)
    return high, (a - high.astype(F32)).astype(BF16)


def triangle(lower):
    row = lax.broadcasted_iota(jnp.int32, (STRETCH, STRETCH), 0)
    column = lax.broadcasted_iota(jnp.int32, (STRETCH, STRETCH), 1)
    return jnp.where(row >= column if lower else row <= column, 1.0, 0.0)


def layer_kernel(
    x_hbm, go_hbm, b_hbm, c_hbm, dt_hbm, start_hbm, al_hbm, sk_hbm, tb_hbm,
    mixed, gx, gb, gc, gdt, grad_a, grad_k, grad_t,
    wide, b_v, c_v, dt_v, start_v, al, sk, tb,
    heads, dt_s, slope_s, cum_s, factor, v_s, masked, enter_s, stay_s, seen_s, seen_t,
    y_s, z_s, gb_s, gc_s, net_s, late_s, end_s, skip_s, weigh_s, ahead_s, early_s,
    ends_here, ends_there, decay, z_decay, part, state, z_in, z_out, up, up_in, down, down_in, params, buf1, buf2,
    in_sem, z_s_sem, z_r_sem, up_s_sem, up_r_sem, down_s_sem, down_r_sem, back_s_sem, back_r_sem,
    s1, r1, s2, r2,
):
    here, dp = lax.axis_index("ctx"), lax.axis_index("dp")
    side, place = lax.rem(here, 2), here // 2
    partner = {"ctx": here + 1 - 2 * side}
    mine_far = dp * 2 + side

    def peer(k):
        return lax.rem(place + k, XY)

    def near(k):
        return {"ctx": peer(k) * 2 + side}

    def far(k):
        g = lax.rem(mine_far + k, FAR)
        return {"dp": g // 2, "ctx": place * 2 + lax.rem(g, 2)}

    loads = []

    def load(src, dst):
        copy = pltpu.make_async_copy(src, dst, in_sem.at[len(loads)])
        copy.start()
        loads.append(copy)
        return copy

    def columns(g):
        return pl.ds(g * GROUP, GROUP)

    def load_wide(d, g):
        return load((x_hbm, go_hbm)[d].at[:, columns(g)], wide.at[d, :, columns(g)])

    small = [load(s, d) for s, d in ((dt_hbm, dt_v), (start_hbm, start_v), (al_hbm, al), (tb_hbm, tb), (sk_hbm, sk))]
    small += [load(b_hbm, b_v), load(c_hbm, c_v)]
    wide_in = [[load_wide(0, 0), load_wide(1, 0)]]

    barrier = pltpu.get_barrier_semaphore()

    def greet_near(k, carry):
        pl.semaphore_signal(barrier, inc=1, device_id=near(k), device_id_type=MESH)
        return carry

    def greet_far(k, carry):
        pl.semaphore_signal(barrier, inc=1, device_id=far(k), device_id_type=MESH)
        return carry

    lax.fori_loop(1, XY, greet_near, 0)
    lax.fori_loop(1, FAR, greet_far, 0)

    def remote(src, dst, send, recv, to):
        return pltpu.make_async_remote_copy(
            src_ref=src, dst_ref=dst, send_sem=send, recv_sem=recv, device_id=to, device_id_type=MESH
        )

    def z_up(g):
        return remote(part.at[1 - side, g], z_in.at[g], z_s_sem.at[0], z_r_sem.at[g], partner)

    def z_decays():
        return remote(ends_here, ends_there, z_s_sem.at[1], z_r_sem.at[G], partner)

    def up_rows(g):
        return pl.ds(8 + g * 2 * BAND, 2 * BAND) if g else pl.ds(0, 8 + 2 * BAND)

    def up_copy(g, k):
        return remote(up.at[peer(k), up_rows(g)], up_in.at[place, up_rows(g)], up_s_sem.at[0], up_r_sem.at[g], near(k))

    def down_rows(g):
        return pl.ds(g * 2 * BAND, 2 * BAND)

    def down_copy(g, k):
        return remote(down.at[peer(k), down_rows(g)], down_in.at[place, down_rows(g)], down_s_sem.at[0], down_r_sem.at[g], near(k))

    def z_back(g):
        return remote(z_out.at[g], state.at[side, g], back_s_sem.at[0], back_r_sem.at[g], partner)

    def received(ref, sem):
        remote(ref, ref, z_s_sem.at[0], sem, partner).wait_recv()

    def sent(ref, sem):
        remote(ref, ref, sem, z_r_sem.at[0], partner).wait_send()

    others = pl.ds(0, XY - 1)

    def each_peer(act):
        def body(k, carry):
            act(k)
            return carry

        lax.fori_loop(1, XY, body, 0)

    def map_heads(g):
        head = lax.broadcasted_iota(jnp.int32, (H, GROUP), 0)
        column = lax.broadcasted_iota(jnp.int32, (H, GROUP), 1) + g * GROUP
        mapped = jnp.where(column // P_SIZE == head, 1.0, 0.0).astype(BF16)
        heads[:H, columns(g)] = mapped
        heads[H:, columns(g)] = mapped

    def expand(values):
        return dot(jnp.concatenate(split(values), axis=1), heads[...])

    map_heads(0)
    lows = triangle(True)
    lows_half = lows.astype(BF16)
    for copy in small:
        copy.wait()
    for g in range(1, G):
        wide_in.append([load_wide(0, g), load_wide(1, g)])
    rate = -jnp.exp(al[...])
    lasts, spans = [], []
    for block in range(2):
        rows = pl.ds(block * STRETCH, STRETCH)
        shifted = jnp.transpose(dt_v[:, block * STRETCH : (block + 1) * STRETCH]) + tb[...]
        tail = jnp.exp(-jnp.abs(shifted))
        dt = jnp.maximum(shifted, 0.0) + jnp.log1p(tail)
        dt_s[rows] = dt
        slope_s[rows] = jnp.where(shifted >= 0.0, 1.0, tail) / (1.0 + tail)
        dt_high, dt_rest = split(dt)
        dt_low = (dt - dt_high.astype(F32) - dt_rest.astype(F32)).astype(BF16)
        cum = rate * (dot(lows_half, dt_high) + dot(lows_half, dt_rest) + dot(lows_half, dt_low))
        cum_s[rows] = cum
        last = cum[STRETCH - 1 :]
        factor[0, rows] = jnp.concatenate(split(jnp.exp(last - cum) * dt), axis=1)
        factor[1, rows] = jnp.concatenate(split(jnp.exp(cum)), axis=1)
        v_s[rows] = jnp.concatenate(split(jnp.exp(-cum) * dt), axis=1)
        start = jnp.broadcast_to(start_v[:, block * STRETCH : (block + 1) * STRETCH].astype(F32), (8, STRETCH))
        start = start.astype(BF16)
        count = dot(lows_half, start, NT)[:, :1]
        spans.append((count, start))
        enters = jnp.where(count == 0.0, 1.0, 0.0)
        stays = jnp.where(count == count[STRETCH - 1 :], 1.0, 0.0)
        masked[0, rows] = (b_v[rows].astype(F32) * stays).astype(BF16)
        masked[1, rows] = (c_v[rows].astype(F32) * enters).astype(BF16)
        enter_s[rows] = jnp.broadcast_to(enters, (STRETCH, N))
        stay_s[rows] = jnp.broadcast_to(stays, (STRETCH, N))
        lasts.append(jnp.exp(last) * jnp.where(count[STRETCH - 1 :] == 0.0, 1.0, 0.0))
    row = lax.broadcasted_iota(jnp.int32, (8, H), 0)
    ends_here[...] = jnp.where(row == 0, lasts[0], jnp.where(row == 1, lasts[1], 0.0))

    def prepare():
        for g in range(1, G):
            map_heads(g)
        for block in range(2):
            rows = pl.ds(block * STRETCH, STRETCH)
            count, start = spans[block]
            same = jnp.where(count == dot(start, lows_half, NT)[:1], 1.0, 0.0)
            seen_s[rows] = same * lows
            seen_t[rows] = same * triangle(False)
        decay[...] = expand(ends_here[...])
        net_s[...] = jnp.zeros_like(net_s)
        late_s[...] = jnp.zeros_like(late_s)
        end_s[...] = jnp.zeros_like(end_s)
        skip_s[...] = jnp.zeros_like(skip_s)

    def narrow(g):
        return slice(g * N, (g + 1) * N)

    def by_head(values, where):
        high, low = split(values)
        return dot(high, where, NT) + dot(low, where, NT)

    def twice(a, axis):
        return jnp.concatenate([a, a], axis=axis)

    def views(g, block):
        rows, cols = pl.ds(block * STRETCH, STRETCH), columns(g)
        u = dot(factor[1, rows], heads[:, cols])
        v = dot(v_s[rows], heads[:, cols])
        x = wide[0, rows, cols].astype(F32)
        go = wide[1, rows, cols].astype(F32)
        return rows, cols, u, v, x, go

    def local(d, g):
        cols = columns(g)
        for block in range(2):
            rows = pl.ds(block * STRETCH, STRETCH)
            scaled = wide[d, rows, cols].astype(F32) * dot(factor[d, rows], heads[:, cols])
            scaled = jnp.concatenate(split(scaled), axis=0)
            part[d, g, lax.rem(block + d, 2)] = dot(twice(masked[d, rows, narrow(g)], 0), scaled, TN)

    def intra(g):
        for block in range(2):
            rows, cols, u, v, x, go = views(g, block)
            b_in, c_in = b_v[rows, narrow(g)], c_v[rows, narrow(g)]
            gu, gu_low = split(go * u)
            xv, xv_low = split(x * v)
            scores, scores_low = split(dot(c_in, b_in, NT) * seen_s[rows])
            back, back_low = split(dot(b_in, c_in, NT) * seen_t[rows])
            y_s[rows, cols] = dot(scores, xv) + dot(scores, xv_low) + dot(scores_low, xv)
            z_s[rows, cols] = dot(back, gu) + dot(back, gu_low) + dot(back_low, gu)
            grad_scores = jnp.where(seen_s[rows] > 0.0, dot(gu, xv, NT), 0.0).astype(BF16)
            gc_s[rows, narrow(g)] = dot(grad_scores, b_in)
            gb_s[rows, narrow(g)] = dot(grad_scores, c_in, TN)
            skips = jnp.sum(x * go, axis=0, keepdims=True)
            skip_s[...] += by_head(jnp.broadcast_to(skips, (8, GROUP)), heads[:H, cols])
            if g == G - 1:
                from_z = x * v * z_s[rows, cols]
                net_s[rows] += by_head(go * u * y_s[rows, cols] - from_z, heads[:H, cols])
                late_s[rows] += by_head(from_z, heads[:H, cols])

    def weigh():
        g = G - 1
        cols = columns(g)
        for block in range(2):
            rows = pl.ds(block * STRETCH, STRETCH)
            x = wide[0, rows, cols].astype(F32)
            go = wide[1, rows, cols].astype(F32)
            cum, slope, dt = cum_s[rows], slope_s[rows], dt_s[rows]
            reach = rate * sum(dot(lows_half, part_slope) for part_slope in split(slope))
            u, k = jnp.exp(cum), jnp.exp(cum[STRETCH - 1 :] - cum) * dt
            plans = ((cum, -cum), (reach, slope / dt - reach))
            for kind, (on_states, on_later) in enumerate(plans):
                ahead = dot(jnp.concatenate(split(u * on_states), axis=1), heads[:, cols]) * go
                behind = dot(jnp.concatenate(split(k * on_later), axis=1), heads[:, cols]) * x
                ahead = jnp.concatenate(split(ahead), axis=0)
                behind = jnp.concatenate(split(behind), axis=0)
                at_end = jnp.broadcast_to(on_states[STRETCH - 1 :], (8, H))
                at_end = dot(jnp.concatenate(split(at_end), axis=1), heads[:, cols])
                weigh_s[kind, block, 0] = dot(twice(masked[1, rows, narrow(g)], 0), ahead, TN)
                weigh_s[kind, block, 1] = (
                    dot(twice(masked[0, rows, narrow(g)], 0), behind, TN) + at_end[:1] * part[0, g, block]
                )
                ahead_s[kind, block] = at_end * decay[block : block + 1, cols]

    def last_sums():
        lines = []
        for kind in range(2):
            line = jnp.zeros((1, GROUP), F32)
            for block in range(2):
                entering, later = state[0, G - 1, block], state[1, G - 1, 1 - block]
                line += jnp.sum(entering * weigh_s[kind, block, 0] + later * weigh_s[kind, block, 1], axis=0, keepdims=True)
                line += ahead_s[kind, block, :1] * jnp.sum(entering * later, axis=0, keepdims=True)
            lines.append(line)
        row = lax.broadcasted_iota(jnp.int32, (8, GROUP), 0)
        lines = jnp.where(row == 0, lines[0], jnp.where(row == 1, lines[1], 0.0))
        return by_head(lines, heads[:H, columns(G - 1)])

    def dt_gradients(block):
        rows = pl.ds(block * STRETCH, STRETCH)
        position = lax.broadcasted_iota(jnp.int32, (STRETCH, H), 0)
        grad_cum = net_s[rows] + jnp.where(position == STRETCH - 1, end_s[block * 8 : block * 8 + 1], 0.0)
        after = dot(triangle(False), grad_cum, precision=lax.Precision.HIGHEST)
        return grad_cum, (late_s[rows] / dt_s[rows] + rate * after) * slope_s[rows]

    def early_sums():
        sum_a = jnp.zeros((1, H), F32)
        sum_t = jnp.zeros((1, H), F32)
        for block in range(2):
            grad_cum, grad_dt = dt_gradients(block)
            sum_a += jnp.sum(cum_s[pl.ds(block * STRETCH, STRETCH)] * grad_cum, axis=0, keepdims=True)
            sum_t += jnp.sum(grad_dt, axis=0, keepdims=True)
        row = lax.broadcasted_iota(jnp.int32, (8, H), 0)
        early_s[...] = jnp.where(row == 0, sum_a, jnp.where(row == 1, sum_t, jnp.where(row == 2, skip_s[:1], 0.0)))

    def final_sums(g):
        for block in range(2):
            rows, cols, u, v, x, go = views(g, block)
            where = heads[:H, cols]
            entering, later = state[0, g, block], state[1, g, 1 - block]
            c_enter = twice(masked[1, rows, narrow(g)], 1)
            b_stay = twice(masked[0, rows, narrow(g)], 1)
            from_state = dot(c_enter, jnp.concatenate(split(entering), axis=0))
            y = y_s[rows, cols] + from_state
            from_later = u[STRETCH - 1 :] * dot(b_stay, jnp.concatenate(split(later), axis=0))
            z = z_s[rows, cols] + from_later
            y_s[rows, cols] = y
            z_s[rows, cols] = z
            xv = x * v
            if g == G - 1:
                y, z = from_state, from_later
            from_z = xv * z
            net_s[rows] += by_head(go * u * y - from_z, where)
            late_s[rows] += by_head(from_z, where)
            ends = jnp.sum(xv * from_later, axis=0, keepdims=True)
            ends += decay[block : block + 1, cols] * jnp.sum(entering * later, axis=0, keepdims=True)
            end_s[block * 8 : (block + 1) * 8] += by_head(jnp.broadcast_to(ends, (8, GROUP)), where)

    def final_out(g):
        skip = skip_row[:, g * GROUP : (g + 1) * GROUP]
        for block in range(2):
            rows, cols, u, v, x, go = views(g, block)
            mixed[rows, cols] = (u * y_s[rows, cols] + skip * x).astype(BF16)
            gx[rows, cols] = (v * z_s[rows, cols] + skip * go).astype(BF16)
            gu = (go * u).astype(BF16)
            xk = (x * (v * u[STRETCH - 1 :])).astype(BF16)
            entering, later = state[0, g, block].astype(BF16), state[1, g, 1 - block].astype(BF16)
            gc[rows, narrow(g)] = (gc_s[rows, narrow(g)] + enter_s[rows] * dot(gu, entering, NT)).astype(BF16)
            gb[rows, narrow(g)] = (gb_s[rows, narrow(g)] + stay_s[rows] * dot(xk, later, NT)).astype(BF16)

    at_zero = side == 0
    first = [at_zero, jnp.logical_not(at_zero)]

    def factors():
        mine = [jnp.where(at_zero, decay[s : s + 1], decay[1 - s : 2 - s]) for s in range(2)]
        theirs = [jnp.where(at_zero, z_decay[s : s + 1], z_decay[1 - s : 2 - s]) for s in range(2)]
        return mine, theirs

    def part_of(row, g):
        return row[:, g * GROUP : (g + 1) * GROUP]

    def combine(g):
        if g == 0:
            z_decays().wait_recv()
            z_decay[...] = expand(ends_there[...])
        z_up(g).wait_recv()
        mine, theirs = factors()
        if g == 0:
            pair = [mine[s] * theirs[s] for s in range(2)]
            for t in range(TILES):
                lines = [
                    pair[s][:, h * GROUP + t * LANES : h * GROUP + (t + 1) * LANES] for h in range(G) for s in range(2)
                ]
                lines = jnp.concatenate(lines, axis=0)
                for o in range(t, XY, TILES):
                    up[o, :8] = lines
        for s in range(2):
            scale_mine = jnp.where(first[s], part_of(theirs[s], g), 1.0)
            scale_theirs = jnp.where(first[s], 1.0, part_of(mine[s], g))
            total = scale_mine * part[side, g, s] + scale_theirs * z_in[g, s]
            for o in range(XY):
                band, t = o // TILES, o % TILES
                up[o, pl.ds(8 + (2 * g + s) * BAND, BAND)] = total[
                    band * BAND : (band + 1) * BAND, t * LANES : (t + 1) * LANES
                ]
        each_peer(lambda k: up_copy(g, k).start())
        up_in[place, up_rows(g)] = up[place, up_rows(g)]

    def scan(g):
        received(up_in.at[others, up_rows(g)], up_r_sem.at[g])

        def rise(j, now):
            down[j, pl.ds(2 * g * BAND, BAND)] = now
            return up_in[j, 2 * g : 2 * g + 1] * now + up_in[j, pl.ds(8 + 2 * g * BAND, BAND)]

        def fall(k, now):
            j = XY - 1 - k
            down[j, pl.ds((2 * g + 1) * BAND, BAND)] = now
            return up_in[j, 2 * g + 1 : 2 * g + 2] * now + up_in[j, pl.ds(8 + (2 * g + 1) * BAND, BAND)]

        now = lax.fori_loop(0, XY, rise, jnp.zeros((BAND, LANES), F32))
        lax.fori_loop(0, XY, fall, now)
        each_peer(lambda k: down_copy(g, k).start())
        down_in[place, down_rows(g)] = down[place, down_rows(g)]

    def spread(g):
        received(down_in.at[others, down_rows(g)], down_r_sem.at[g])
        mine, theirs = factors()
        for s in range(2):
            at = pl.ds((2 * g + s) * BAND, BAND)
            enter = jnp.concatenate(
                [
                    jnp.concatenate([down_in[r * TILES + t, at] for t in range(TILES)], axis=1)
                    for r in range(XY // TILES)
                ],
                axis=0,
            )
            keep = jnp.where(first[s], 1.0, part_of(theirs[s], g))
            keep_add = jnp.where(first[s], 0.0, 1.0)
            give = jnp.where(first[s], part_of(mine[s], g), 1.0)
            give_add = jnp.where(first[s], 1.0, 0.0)
            z_out[g, s] = give * enter + give_add * part[side, g, s]
            state[side, g, s] = keep * enter + keep_add * z_in[g, s]
        z_back(g).start()

    for copy in wide_in[0]:
        copy.wait()
    local(1 - side, 0)
    pl.semaphore_wait(barrier, XY + FAR - 2)
    z_decays().start()
    z_up(0).start()
    prepare()
    skip_row = expand(jnp.broadcast_to(sk[...], (8, H)))[:1]
    for g in range(1, G):
        for copy in wide_in[g]:
            copy.wait()
        local(1 - side, g)
        z_up(g).start()
    for g in range(G):
        local(side, g)
    for g in range(G):
        intra(g)
        combine(g)
        if g >= 1:
            scan(g - 1)
        if g >= 2:
            spread(g - 2)
    scan(G - 1)
    spread(G - 2)
    z_back(0).wait_recv()
    final_sums(0)
    spread(G - 1)
    final_out(0)
    z_decays().wait_send()
    sent(z_in, z_s_sem.at[0])
    sent(up.at[others], up_s_sem.at[0])
    sent(down.at[others], down_s_sem.at[0])
    weigh()
    for g in range(1, G - 1):
        z_back(g).wait_recv()
        final_sums(g)
        final_out(g)
    early_sums()
    sent(z_out, back_s_sem.at[0])
    z_back(G - 1).wait_recv()
    params[...] = early_s[...] + last_sums()

    def sum1(k):
        return remote(params, buf2.at[k], s2.at[0], r2.at[0], far(k))

    def sum2(k):
        return remote(buf1.at[0], buf1.at[k], s1.at[0], r1.at[0], near(k))

    def each_far(act):
        def body(k, carry):
            act(k)
            return carry

        lax.fori_loop(1, FAR, body, 0)

    each_far(lambda k: sum1(k).start())
    buf2[0] = params[...]
    final_sums(G - 1)
    received(buf2.at[pl.ds(1, FAR - 1)], r2.at[0])
    total = jnp.zeros((8, H), F32)
    for g in range(FAR):
        total += buf2[lax.rem(mine_far - g + FAR, FAR)]
    buf1[0] = total
    each_peer(lambda k: sum2(k).start())
    final_out(G - 1)
    for block in range(2):
        gdt[:, block * STRETCH : (block + 1) * STRETCH] = jnp.transpose(dt_gradients(block)[1])
    sent(buf2.at[pl.ds(1, FAR - 1)], s2.at[0])
    received(buf1.at[pl.ds(1, XY - 1)], r1.at[0])
    total = jnp.zeros((8, H), F32)
    for g in range(XY):
        total += buf1[lax.rem(place - g + XY, XY)]
    grad_a[...] = total[0:1]
    grad_t[...] = total[1:2]
    grad_k[...] = total[2:3]
    sent(buf1.at[pl.ds(1, XY - 1)], s1.at[0])


def store_kernel(*refs):
    count = len(refs) // 2
    sems = refs[-1]
    copies = []
    for src, dst in zip(refs[:count], refs[count:]):
        pieces = PIECES if src.shape[0] == ROWS else 1
        for i in range(pieces):
            rows = pl.ds(i * (src.shape[0] // pieces), src.shape[0] // pieces)
            copy = pltpu.make_async_copy(src.at[rows], dst.at[rows], sems.at[len(copies)])
            copy.start()
            copies.append(copy)
    for copy in copies:
        copy.wait()


def shards(hidden_x, b_proj, c_proj, dt_raw, span_start, a_log, skip_gain, dt_bias, out_grad):
    arrays = (
        hidden_x.reshape(ROWS, WIDTH),
        out_grad.reshape(ROWS, WIDTH),
        b_proj.reshape(ROWS, G * N),
        c_proj.reshape(ROWS, G * N),
        dt_raw.reshape(ROWS, H).T,
        span_start.reshape(1, ROWS),
        a_log.reshape(1, H),
        skip_gain.reshape(1, H),
        dt_bias.reshape(1, H),
    )
    anywhere = pl.BlockSpec(memory_space=pltpu.HBM)
    vmem = pl.BlockSpec(memory_space=pltpu.VMEM)
    dma = pltpu.SemaphoreType.DMA

    def f32(*shape):
        return pltpu.VMEM(shape, F32)

    def bf16(*shape):
        return pltpu.VMEM(shape, BF16)

    wide = jax.ShapeDtypeStruct((ROWS, WIDTH), BF16)
    slim = jax.ShapeDtypeStruct((ROWS, G * N), BF16)
    line = jax.ShapeDtypeStruct((1, H), F32)
    outs = (wide, wide, slim, slim, jax.ShapeDtypeStruct((H, ROWS), F32), line, line, line)
    held = tuple(pltpu.VMEM(out.shape, out.dtype) for out in outs)
    arrays = [pltpu.with_memory_space_constraint(a, pltpu.HBM) for a in arrays]
    results = pl.pallas_call(
        layer_kernel,
        out_shape=held,
        in_specs=[anywhere] * len(arrays),
        out_specs=(vmem,) * len(outs),
        scratch_shapes=[
            bf16(2, ROWS, WIDTH), bf16(ROWS, G * N), bf16(ROWS, G * N), f32(H, ROWS),
            pltpu.VMEM((1, ROWS), jnp.int32), f32(1, H), f32(1, H), f32(1, H),
            bf16(2 * H, WIDTH), f32(ROWS, H), f32(ROWS, H), f32(ROWS, H), bf16(2, ROWS, 2 * H), bf16(ROWS, 2 * H),
            bf16(2, ROWS, G * N), f32(ROWS, N), f32(ROWS, N), f32(ROWS, STRETCH), f32(ROWS, STRETCH),
            f32(ROWS, WIDTH), f32(ROWS, WIDTH),
            f32(ROWS, G * N), f32(ROWS, G * N), f32(ROWS, H), f32(ROWS, H), f32(16, H), f32(8, H),
            f32(2, 2, 2, N, GROUP), f32(2, 2, 8, GROUP), f32(8, H),
            f32(8, H), f32(8, H), f32(8, WIDTH), f32(8, WIDTH),
            f32(2, G, 2, N, GROUP), f32(2, G, 2, N, GROUP), f32(G, 2, N, GROUP), f32(G, 2, N, GROUP),
            f32(XY, 8 + 2 * N, LANES), f32(XY, 8 + 2 * N, LANES), f32(XY, 2 * N, LANES), f32(XY, 2 * N, LANES),
            f32(8, H), f32(XY, 8, H), f32(FAR, 8, H),
            dma((7 + 2 * G,)), dma((2,)), dma((G + 1,)),
            dma((1,)), dma((G,)), dma((1,)), dma((G,)), dma((1,)), dma((G,)),
            dma((1,)), dma((1,)), dma((1,)), dma((1,)),
        ],
        compiler_params=pltpu.CompilerParams(
            collective_id=0, has_side_effects=True, vmem_limit_bytes=44 * 2**20
        ),
        cost_estimate=pl.CostEstimate(flops=5 * 10**9, bytes_accessed=10 * 2**20, transcendentals=10**5),
        name="layer",
    )(*arrays)
    mixed, gx, gb, gc, gdt, grad_a, grad_k, grad_t = pl.pallas_call(
        store_kernel,
        out_shape=outs,
        in_specs=[vmem] * len(outs),
        out_specs=(anywhere,) * len(outs),
        scratch_shapes=[dma((4 * PIECES + 4,))],
        compiler_params=pltpu.CompilerParams(vmem_limit_bytes=2**20),
        name="store",
    )(*[pltpu.with_memory_space_constraint(r, pltpu.VMEM) for r in results])
    return (
        mixed.reshape(1, ROWS, WIDTH),
        gx.reshape(1, ROWS, WIDTH),
        gb.reshape(1, ROWS, G * N),
        gc.reshape(1, ROWS, G * N),
        gdt.T.reshape(1, ROWS, H),
        grad_a.reshape(H),
        grad_k.reshape(H),
        grad_t.reshape(H),
    )


def solution(mesh):
    rows = P("dp", "ctx", None)
    return jax.shard_map(
        shards,
        mesh=mesh,
        in_specs=(rows, rows, rows, rows, P("dp", "ctx"), P(), P(), P(), rows),
        out_specs=(rows, rows, rows, rows, rows, P(), P(), P()),
        check_vma=False,
    )
```

```python
import jax
import jax.numpy as jnp
from jax import lax
from jax.experimental import pallas as pl
from jax.experimental.pallas import tpu as pltpu
from jax.sharding import PartitionSpec as P

H = 64
P_SIZE = 32
N = 64
G = 4
STRETCH = 256
ROWS = 2 * STRETCH
WIDTH = H * P_SIZE
GROUP = WIDTH // G
XY = 16
LANES = 128
TILES = GROUP // LANES
BAND = N // (XY // TILES)
FAR = 8
PIECES = 4
F32 = jnp.float32
BF16 = jnp.bfloat16
MESH = pl.DeviceIdType.MESH
NN = ((1,), (0,))
NT = ((1,), (1,))
TN = ((0,), (0,))


def dot(a, b, dims=NN, precision=None):
    return lax.dot_general(a, b, (dims, ((), ())), preferred_element_type=F32, precision=precision)


def split(a):
    high = a.astype(BF16)
    return high, (a - high.astype(F32)).astype(BF16)


def triangle(lower):
    row = lax.broadcasted_iota(jnp.int32, (STRETCH, STRETCH), 0)
    column = lax.broadcasted_iota(jnp.int32, (STRETCH, STRETCH), 1)
    return jnp.where(row >= column if lower else row <= column, 1.0, 0.0)


def layer_kernel(
    x_hbm, go_hbm, b_hbm, c_hbm, dt_hbm, start_hbm, al_hbm, sk_hbm, tb_hbm,
    mixed, gx, gb, gc, gdt, grad_a, grad_k, grad_t,
    wide, b_v, c_v, dt_v, start_v, al, sk, tb,
    heads, dt_s, slope_s, cum_s, factor, v_s, masked, enter_s, stay_s, seen_s, seen_t,
    y_s, z_s, gb_s, gc_s, net_s, late_s, end_s, skip_s, weigh_s, ahead_s, early_s,
    ends_here, ends_there, decay, z_decay, part, state, z_in, z_out, up, up_in, down, down_in, params, buf1, buf2,
    in_sem, z_s_sem, z_r_sem, up_s_sem, up_r_sem, down_s_sem, down_r_sem, back_s_sem, back_r_sem,
    s1, r1, s2, r2,
):
    here, dp = lax.axis_index("ctx"), lax.axis_index("dp")
    side, place = lax.rem(here, 2), here // 2
    partner = {"ctx": here + 1 - 2 * side}
    mine_far = dp * 2 + side

    def peer(k):
        return lax.rem(place + k, XY)

    def near(k):
        return {"ctx": peer(k) * 2 + side}

    def far(k):
        g = lax.rem(mine_far + k, FAR)
        return {"dp": g // 2, "ctx": place * 2 + lax.rem(g, 2)}

    barrier = pltpu.get_barrier_semaphore()

    def greet_near(k, carry):
        pl.semaphore_signal(barrier, inc=1, device_id=near(k), device_id_type=MESH)
        return carry

    def greet_far(k, carry):
        pl.semaphore_signal(barrier, inc=1, device_id=far(k), device_id_type=MESH)
        return carry

    lax.fori_loop(1, FAR, greet_far, 0)
    lax.fori_loop(1, XY, greet_near, 0)

    loads = []

    def load(src, dst):
        copy = pltpu.make_async_copy(src, dst, in_sem.at[len(loads)])
        copy.start()
        loads.append(copy)
        return copy

    def columns(g):
        return pl.ds(g * GROUP, GROUP)

    def load_wide(d, g):
        return load((x_hbm, go_hbm)[d].at[:, columns(g)], wide.at[d, :, columns(g)])

    small = [load(s, d) for s, d in ((dt_hbm, dt_v), (start_hbm, start_v), (al_hbm, al), (tb_hbm, tb), (sk_hbm, sk))]
    small += [load(b_hbm, b_v), load(c_hbm, c_v)]
    wide_in = [[load_wide(0, 0), load_wide(1, 0)]]

    def remote(src, dst, send, recv, to):
        return pltpu.make_async_remote_copy(
            src_ref=src, dst_ref=dst, send_sem=send, recv_sem=recv, device_id=to, device_id_type=MESH
        )

    def z_up(g):
        return remote(part.at[1 - side, g], z_in.at[g], z_s_sem.at[0], z_r_sem.at[g], partner)

    def z_decays():
        return remote(ends_here, ends_there, z_s_sem.at[1], z_r_sem.at[G], partner)

    def up_rows(g):
        return pl.ds(8 + g * 2 * BAND, 2 * BAND) if g else pl.ds(0, 8 + 2 * BAND)

    def up_copy(g, k):
        return remote(up.at[peer(k), up_rows(g)], up_in.at[place, up_rows(g)], up_s_sem.at[0], up_r_sem.at[g], near(k))

    def down_rows(g):
        return pl.ds(g * 2 * BAND, 2 * BAND)

    def down_copy(g, k):
        return remote(down.at[peer(k), down_rows(g)], down_in.at[place, down_rows(g)], down_s_sem.at[0], down_r_sem.at[g], near(k))

    def z_back(g):
        return remote(z_out.at[g], state.at[side, g], back_s_sem.at[0], back_r_sem.at[g], partner)

    def received(ref, sem):
        remote(ref, ref, z_s_sem.at[0], sem, partner).wait_recv()

    def sent(ref, sem):
        remote(ref, ref, sem, z_r_sem.at[0], partner).wait_send()

    others = pl.ds(0, XY - 1)

    def each_peer(act):
        def body(k, carry):
            act(k)
            return carry

        lax.fori_loop(1, XY, body, 0)

    def map_heads(g):
        head = lax.broadcasted_iota(jnp.int32, (H, GROUP), 0)
        column = lax.broadcasted_iota(jnp.int32, (H, GROUP), 1) + g * GROUP
        mapped = jnp.where(column // P_SIZE == head, 1.0, 0.0).astype(BF16)
        heads[:H, columns(g)] = mapped
        heads[H:, columns(g)] = mapped

    def expand(values):
        return dot(jnp.concatenate(split(values), axis=1), heads[...])

    map_heads(0)
    lows = triangle(True)
    lows_half = lows.astype(BF16)
    for copy in small:
        copy.wait()
    for g in range(1, G):
        wide_in.append([load_wide(0, g), load_wide(1, g)])
    rate = -jnp.exp(al[...])
    lasts, spans = [], []
    for block in range(2):
        rows = pl.ds(block * STRETCH, STRETCH)
        shifted = jnp.transpose(dt_v[:, block * STRETCH : (block + 1) * STRETCH]) + tb[...]
        tail = jnp.exp(-jnp.abs(shifted))
        dt = jnp.maximum(shifted, 0.0) + jnp.log1p(tail)
        dt_s[rows] = dt
        slope_s[rows] = jnp.where(shifted >= 0.0, 1.0, tail) / (1.0 + tail)
        dt_high, dt_rest = split(dt)
        dt_low = (dt - dt_high.astype(F32) - dt_rest.astype(F32)).astype(BF16)
        cum = rate * (dot(lows_half, dt_high) + dot(lows_half, dt_rest) + dot(lows_half, dt_low))
        cum_s[rows] = cum
        last = cum[STRETCH - 1 :]
        factor[0, rows] = jnp.concatenate(split(jnp.exp(last - cum) * dt), axis=1)
        factor[1, rows] = jnp.concatenate(split(jnp.exp(cum)), axis=1)
        v_s[rows] = jnp.concatenate(split(jnp.exp(-cum) * dt), axis=1)
        start = jnp.broadcast_to(start_v[:, block * STRETCH : (block + 1) * STRETCH].astype(F32), (8, STRETCH))
        start = start.astype(BF16)
        count = dot(lows_half, start, NT)[:, :1]
        spans.append((count, start))
        enters = jnp.where(count == 0.0, 1.0, 0.0)
        stays = jnp.where(count == count[STRETCH - 1 :], 1.0, 0.0)
        masked[0, rows] = (b_v[rows].astype(F32) * stays).astype(BF16)
        masked[1, rows] = (c_v[rows].astype(F32) * enters).astype(BF16)
        enter_s[rows] = jnp.broadcast_to(enters, (STRETCH, N))
        stay_s[rows] = jnp.broadcast_to(stays, (STRETCH, N))
        lasts.append(jnp.exp(last) * jnp.where(count[STRETCH - 1 :] == 0.0, 1.0, 0.0))
    row = lax.broadcasted_iota(jnp.int32, (8, H), 0)
    ends_here[...] = jnp.where(row == 0, lasts[0], jnp.where(row == 1, lasts[1], 0.0))

    def prepare():
        for g in range(1, G):
            map_heads(g)
        for block in range(2):
            rows = pl.ds(block * STRETCH, STRETCH)
            count, start = spans[block]
            same = jnp.where(count == dot(start, lows_half, NT)[:1], 1.0, 0.0)
            seen_s[rows] = same * lows
            seen_t[rows] = same * triangle(False)
        decay[...] = expand(ends_here[...])
        net_s[...] = jnp.zeros_like(net_s)
        late_s[...] = jnp.zeros_like(late_s)
        end_s[...] = jnp.zeros_like(end_s)
        skip_s[...] = jnp.zeros_like(skip_s)

    def narrow(g):
        return slice(g * N, (g + 1) * N)

    def by_head(values, where):
        high, low = split(values)
        return dot(high, where, NT) + dot(low, where, NT)

    def twice(a, axis):
        return jnp.concatenate([a, a], axis=axis)

    def views(g, block):
        rows, cols = pl.ds(block * STRETCH, STRETCH), columns(g)
        u = dot(factor[1, rows], heads[:, cols])
        v = dot(v_s[rows], heads[:, cols])
        x = wide[0, rows, cols].astype(F32)
        go = wide[1, rows, cols].astype(F32)
        return rows, cols, u, v, x, go

    def local(d, g):
        cols = columns(g)
        for block in range(2):
            rows = pl.ds(block * STRETCH, STRETCH)
            scaled = wide[d, rows, cols].astype(F32) * dot(factor[d, rows], heads[:, cols])
            scaled = jnp.concatenate(split(scaled), axis=0)
            part[d, g, lax.rem(block + d, 2)] = dot(twice(masked[d, rows, narrow(g)], 0), scaled, TN)

    def intra(g):
        for block in range(2):
            rows, cols, u, v, x, go = views(g, block)
            b_in, c_in = b_v[rows, narrow(g)], c_v[rows, narrow(g)]
            gu, gu_low = split(go * u)
            xv, xv_low = split(x * v)
            scores, scores_low = split(dot(c_in, b_in, NT) * seen_s[rows])
            back, back_low = split(dot(b_in, c_in, NT) * seen_t[rows])
            y_s[rows, cols] = dot(scores, xv) + dot(scores, xv_low) + dot(scores_low, xv)
            z_s[rows, cols] = dot(back, gu) + dot(back, gu_low) + dot(back_low, gu)
            grad_scores = jnp.where(seen_s[rows] > 0.0, dot(gu, xv, NT), 0.0).astype(BF16)
            gc_s[rows, narrow(g)] = dot(grad_scores, b_in)
            gb_s[rows, narrow(g)] = dot(grad_scores, c_in, TN)
            skips = jnp.sum(x * go, axis=0, keepdims=True)
            skip_s[...] += by_head(jnp.broadcast_to(skips, (8, GROUP)), heads[:H, cols])
            if g == G - 1:
                from_z = x * v * z_s[rows, cols]
                net_s[rows] += by_head(go * u * y_s[rows, cols] - from_z, heads[:H, cols])
                late_s[rows] += by_head(from_z, heads[:H, cols])

    def weigh():
        g = G - 1
        cols = columns(g)
        for block in range(2):
            rows = pl.ds(block * STRETCH, STRETCH)
            x = wide[0, rows, cols].astype(F32)
            go = wide[1, rows, cols].astype(F32)
            cum, slope, dt = cum_s[rows], slope_s[rows], dt_s[rows]
            reach = rate * sum(dot(lows_half, part_slope) for part_slope in split(slope))
            u, k = jnp.exp(cum), jnp.exp(cum[STRETCH - 1 :] - cum) * dt
            plans = ((cum, -cum), (reach, slope / dt - reach))
            for kind, (on_states, on_later) in enumerate(plans):
                ahead = dot(jnp.concatenate(split(u * on_states), axis=1), heads[:, cols]) * go
                behind = dot(jnp.concatenate(split(k * on_later), axis=1), heads[:, cols]) * x
                ahead = jnp.concatenate(split(ahead), axis=0)
                behind = jnp.concatenate(split(behind), axis=0)
                at_end = jnp.broadcast_to(on_states[STRETCH - 1 :], (8, H))
                at_end = dot(jnp.concatenate(split(at_end), axis=1), heads[:, cols])
                weigh_s[kind, block, 0] = dot(twice(masked[1, rows, narrow(g)], 0), ahead, TN)
                weigh_s[kind, block, 1] = (
                    dot(twice(masked[0, rows, narrow(g)], 0), behind, TN) + at_end[:1] * part[0, g, block]
                )
                ahead_s[kind, block] = at_end * decay[block : block + 1, cols]

    def last_sums():
        lines = []
        for kind in range(2):
            line = jnp.zeros((1, GROUP), F32)
            for block in range(2):
                entering, later = state[0, G - 1, block], state[1, G - 1, 1 - block]
                line += jnp.sum(entering * weigh_s[kind, block, 0] + later * weigh_s[kind, block, 1], axis=0, keepdims=True)
                line += ahead_s[kind, block, :1] * jnp.sum(entering * later, axis=0, keepdims=True)
            lines.append(line)
        row = lax.broadcasted_iota(jnp.int32, (8, GROUP), 0)
        lines = jnp.where(row == 0, lines[0], jnp.where(row == 1, lines[1], 0.0))
        return by_head(lines, heads[:H, columns(G - 1)])

    def dt_gradients(block):
        rows = pl.ds(block * STRETCH, STRETCH)
        position = lax.broadcasted_iota(jnp.int32, (STRETCH, H), 0)
        grad_cum = net_s[rows] + jnp.where(position == STRETCH - 1, end_s[block * 8 : block * 8 + 1], 0.0)
        after = dot(triangle(False), grad_cum, precision=lax.Precision.HIGHEST)
        return grad_cum, (late_s[rows] / dt_s[rows] + rate * after) * slope_s[rows]

    def early_sums():
        sum_a = jnp.zeros((1, H), F32)
        sum_t = jnp.zeros((1, H), F32)
        for block in range(2):
            grad_cum, grad_dt = dt_gradients(block)
            sum_a += jnp.sum(cum_s[pl.ds(block * STRETCH, STRETCH)] * grad_cum, axis=0, keepdims=True)
            sum_t += jnp.sum(grad_dt, axis=0, keepdims=True)
        row = lax.broadcasted_iota(jnp.int32, (8, H), 0)
        early_s[...] = jnp.where(row == 0, sum_a, jnp.where(row == 1, sum_t, jnp.where(row == 2, skip_s[:1], 0.0)))

    def final_sums(g):
        for block in range(2):
            rows, cols, u, v, x, go = views(g, block)
            where = heads[:H, cols]
            entering, later = state[0, g, block], state[1, g, 1 - block]
            c_enter = twice(masked[1, rows, narrow(g)], 1)
            b_stay = twice(masked[0, rows, narrow(g)], 1)
            from_state = dot(c_enter, jnp.concatenate(split(entering), axis=0))
            y = y_s[rows, cols] + from_state
            from_later = u[STRETCH - 1 :] * dot(b_stay, jnp.concatenate(split(later), axis=0))
            z = z_s[rows, cols] + from_later
            y_s[rows, cols] = y
            z_s[rows, cols] = z
            xv = x * v
            if g == G - 1:
                y, z = from_state, from_later
            from_z = xv * z
            net_s[rows] += by_head(go * u * y - from_z, where)
            late_s[rows] += by_head(from_z, where)
            ends = jnp.sum(xv * from_later, axis=0, keepdims=True)
            ends += decay[block : block + 1, cols] * jnp.sum(entering * later, axis=0, keepdims=True)
            end_s[block * 8 : (block + 1) * 8] += by_head(jnp.broadcast_to(ends, (8, GROUP)), where)

    def final_out(g):
        skip = skip_row[:, g * GROUP : (g + 1) * GROUP]
        for block in range(2):
            rows, cols, u, v, x, go = views(g, block)
            mixed[rows, cols] = (u * y_s[rows, cols] + skip * x).astype(BF16)
            gx[rows, cols] = (v * z_s[rows, cols] + skip * go).astype(BF16)
            gu = (go * u).astype(BF16)
            xk = (x * (v * u[STRETCH - 1 :])).astype(BF16)
            entering, later = state[0, g, block].astype(BF16), state[1, g, 1 - block].astype(BF16)
            gc[rows, narrow(g)] = (gc_s[rows, narrow(g)] + enter_s[rows] * dot(gu, entering, NT)).astype(BF16)
            gb[rows, narrow(g)] = (gb_s[rows, narrow(g)] + stay_s[rows] * dot(xk, later, NT)).astype(BF16)

    at_zero = side == 0
    first = [at_zero, jnp.logical_not(at_zero)]

    def factors():
        mine = [jnp.where(at_zero, decay[s : s + 1], decay[1 - s : 2 - s]) for s in range(2)]
        theirs = [jnp.where(at_zero, z_decay[s : s + 1], z_decay[1 - s : 2 - s]) for s in range(2)]
        return mine, theirs

    def part_of(row, g):
        return row[:, g * GROUP : (g + 1) * GROUP]

    def combine(g):
        if g == 0:
            z_decays().wait_recv()
            z_decay[...] = expand(ends_there[...])
        z_up(g).wait_recv()
        mine, theirs = factors()
        if g == 0:
            pair = [mine[s] * theirs[s] for s in range(2)]
            for t in range(TILES):
                lines = [
                    pair[s][:, h * GROUP + t * LANES : h * GROUP + (t + 1) * LANES] for h in range(G) for s in range(2)
                ]
                lines = jnp.concatenate(lines, axis=0)
                for o in range(t, XY, TILES):
                    up[o, :8] = lines
        for s in range(2):
            scale_mine = jnp.where(first[s], part_of(theirs[s], g), 1.0)
            scale_theirs = jnp.where(first[s], 1.0, part_of(mine[s], g))
            total = scale_mine * part[side, g, s] + scale_theirs * z_in[g, s]
            for o in range(XY):
                band, t = o // TILES, o % TILES
                up[o, pl.ds(8 + (2 * g + s) * BAND, BAND)] = total[
                    band * BAND : (band + 1) * BAND, t * LANES : (t + 1) * LANES
                ]
        each_peer(lambda k: up_copy(g, k).start())
        up_in[place, up_rows(g)] = up[place, up_rows(g)]

    def scan(g):
        received(up_in.at[others, up_rows(g)], up_r_sem.at[g])

        def rise(j, now):
            down[j, pl.ds(2 * g * BAND, BAND)] = now
            return up_in[j, 2 * g : 2 * g + 1] * now + up_in[j, pl.ds(8 + 2 * g * BAND, BAND)]

        def fall(k, now):
            j = XY - 1 - k
            down[j, pl.ds((2 * g + 1) * BAND, BAND)] = now
            return up_in[j, 2 * g + 1 : 2 * g + 2] * now + up_in[j, pl.ds(8 + (2 * g + 1) * BAND, BAND)]

        now = lax.fori_loop(0, XY, rise, jnp.zeros((BAND, LANES), F32))
        lax.fori_loop(0, XY, fall, now)
        each_peer(lambda k: down_copy(g, k).start())
        down_in[place, down_rows(g)] = down[place, down_rows(g)]

    def spread(g):
        received(down_in.at[others, down_rows(g)], down_r_sem.at[g])
        mine, theirs = factors()
        for s in range(2):
            at = pl.ds((2 * g + s) * BAND, BAND)
            enter = jnp.concatenate(
                [
                    jnp.concatenate([down_in[r * TILES + t, at] for t in range(TILES)], axis=1)
                    for r in range(XY // TILES)
                ],
                axis=0,
            )
            keep = jnp.where(first[s], 1.0, part_of(theirs[s], g))
            keep_add = jnp.where(first[s], 0.0, 1.0)
            give = jnp.where(first[s], part_of(mine[s], g), 1.0)
            give_add = jnp.where(first[s], 1.0, 0.0)
            z_out[g, s] = give * enter + give_add * part[side, g, s]
            state[side, g, s] = keep * enter + keep_add * z_in[g, s]
        z_back(g).start()

    for copy in wide_in[0]:
        copy.wait()
    local(1 - side, 0)
    pl.semaphore_wait(barrier, XY + FAR - 2)
    z_decays().start()
    z_up(0).start()
    prepare()
    skip_row = expand(jnp.broadcast_to(sk[...], (8, H)))[:1]
    for g in range(1, G):
        for copy in wide_in[g]:
            copy.wait()
        local(1 - side, g)
        z_up(g).start()
    for g in range(G):
        local(side, g)
    for g in range(G):
        intra(g)
        combine(g)
        if g >= 1:
            scan(g - 1)
        if g >= 2:
            spread(g - 2)
    scan(G - 1)
    spread(G - 2)
    z_back(0).wait_recv()
    final_sums(0)
    spread(G - 1)
    final_out(0)
    z_decays().wait_send()
    sent(z_in, z_s_sem.at[0])
    sent(up.at[others], up_s_sem.at[0])
    sent(down.at[others], down_s_sem.at[0])
    weigh()
    for g in range(1, G - 1):
        z_back(g).wait_recv()
        final_sums(g)
        final_out(g)
    early_sums()
    sent(z_out, back_s_sem.at[0])
    z_back(G - 1).wait_recv()
    params[...] = early_s[...] + last_sums()

    def sum1(k):
        return remote(params, buf2.at[k], s2.at[0], r2.at[0], far(k))

    def sum2(k):
        return remote(buf1.at[0], buf1.at[k], s1.at[0], r1.at[0], near(k))

    def each_far(act):
        def body(k, carry):
            act(k)
            return carry

        lax.fori_loop(1, FAR, body, 0)

    each_far(lambda k: sum1(k).start())
    buf2[0] = params[...]
    final_sums(G - 1)
    received(buf2.at[pl.ds(1, FAR - 1)], r2.at[0])
    total = jnp.zeros((8, H), F32)
    for g in range(FAR):
        total += buf2[lax.rem(mine_far - g + FAR, FAR)]
    buf1[0] = total
    each_peer(lambda k: sum2(k).start())
    final_out(G - 1)
    for block in range(2):
        gdt[:, block * STRETCH : (block + 1) * STRETCH] = jnp.transpose(dt_gradients(block)[1])
    sent(buf2.at[pl.ds(1, FAR - 1)], s2.at[0])
    received(buf1.at[pl.ds(1, XY - 1)], r1.at[0])
    total = jnp.zeros((8, H), F32)
    for g in range(XY):
        total += buf1[lax.rem(place - g + XY, XY)]
    grad_a[...] = total[0:1]
    grad_t[...] = total[1:2]
    grad_k[...] = total[2:3]
    sent(buf1.at[pl.ds(1, XY - 1)], s1.at[0])


def store_kernel(*refs):
    count = len(refs) // 2
    sems = refs[-1]
    copies = []
    for src, dst in zip(refs[:count], refs[count:]):
        pieces = PIECES if src.shape[0] == ROWS else 1
        for i in range(pieces):
            rows = pl.ds(i * (src.shape[0] // pieces), src.shape[0] // pieces)
            copy = pltpu.make_async_copy(src.at[rows], dst.at[rows], sems.at[len(copies)])
            copy.start()
            copies.append(copy)
    for copy in copies:
        copy.wait()


def shards(hidden_x, b_proj, c_proj, dt_raw, span_start, a_log, skip_gain, dt_bias, out_grad):
    arrays = (
        hidden_x.reshape(ROWS, WIDTH),
        out_grad.reshape(ROWS, WIDTH),
        b_proj.reshape(ROWS, G * N),
        c_proj.reshape(ROWS, G * N),
        dt_raw.reshape(ROWS, H).T,
        span_start.reshape(1, ROWS),
        a_log.reshape(1, H),
        skip_gain.reshape(1, H),
        dt_bias.reshape(1, H),
    )
    anywhere = pl.BlockSpec(memory_space=pltpu.HBM)
    vmem = pl.BlockSpec(memory_space=pltpu.VMEM)
    dma = pltpu.SemaphoreType.DMA

    def f32(*shape):
        return pltpu.VMEM(shape, F32)

    def bf16(*shape):
        return pltpu.VMEM(shape, BF16)

    wide = jax.ShapeDtypeStruct((ROWS, WIDTH), BF16)
    slim = jax.ShapeDtypeStruct((ROWS, G * N), BF16)
    line = jax.ShapeDtypeStruct((1, H), F32)
    outs = (wide, wide, slim, slim, jax.ShapeDtypeStruct((H, ROWS), F32), line, line, line)
    held = tuple(pltpu.VMEM(out.shape, out.dtype) for out in outs)
    arrays = [pltpu.with_memory_space_constraint(a, pltpu.HBM) for a in arrays]
    results = pl.pallas_call(
        layer_kernel,
        out_shape=held,
        in_specs=[anywhere] * len(arrays),
        out_specs=(vmem,) * len(outs),
        scratch_shapes=[
            bf16(2, ROWS, WIDTH), bf16(ROWS, G * N), bf16(ROWS, G * N), f32(H, ROWS),
            pltpu.VMEM((1, ROWS), jnp.int32), f32(1, H), f32(1, H), f32(1, H),
            bf16(2 * H, WIDTH), f32(ROWS, H), f32(ROWS, H), f32(ROWS, H), bf16(2, ROWS, 2 * H), bf16(ROWS, 2 * H),
            bf16(2, ROWS, G * N), f32(ROWS, N), f32(ROWS, N), f32(ROWS, STRETCH), f32(ROWS, STRETCH),
            f32(ROWS, WIDTH), f32(ROWS, WIDTH),
            f32(ROWS, G * N), f32(ROWS, G * N), f32(ROWS, H), f32(ROWS, H), f32(16, H), f32(8, H),
            f32(2, 2, 2, N, GROUP), f32(2, 2, 8, GROUP), f32(8, H),
            f32(8, H), f32(8, H), f32(8, WIDTH), f32(8, WIDTH),
            f32(2, G, 2, N, GROUP), f32(2, G, 2, N, GROUP), f32(G, 2, N, GROUP), f32(G, 2, N, GROUP),
            f32(XY, 8 + 2 * N, LANES), f32(XY, 8 + 2 * N, LANES), f32(XY, 2 * N, LANES), f32(XY, 2 * N, LANES),
            f32(8, H), f32(XY, 8, H), f32(FAR, 8, H),
            dma((7 + 2 * G,)), dma((2,)), dma((G + 1,)),
            dma((1,)), dma((G,)), dma((1,)), dma((G,)), dma((1,)), dma((G,)),
            dma((1,)), dma((1,)), dma((1,)), dma((1,)),
        ],
        compiler_params=pltpu.CompilerParams(
            collective_id=0, has_side_effects=True, vmem_limit_bytes=44 * 2**20
        ),
        cost_estimate=pl.CostEstimate(flops=5 * 10**9, bytes_accessed=10 * 2**20, transcendentals=10**5),
        name="layer",
    )(*arrays)
    mixed, gx, gb, gc, gdt, grad_a, grad_k, grad_t = pl.pallas_call(
        store_kernel,
        out_shape=outs,
        in_specs=[vmem] * len(outs),
        out_specs=(anywhere,) * len(outs),
        scratch_shapes=[dma((4 * PIECES + 4,))],
        compiler_params=pltpu.CompilerParams(vmem_limit_bytes=2**20),
        name="store",
    )(*[pltpu.with_memory_space_constraint(r, pltpu.VMEM) for r in results])
    return (
        mixed.reshape(1, ROWS, WIDTH),
        gx.reshape(1, ROWS, WIDTH),
        gb.reshape(1, ROWS, G * N),
        gc.reshape(1, ROWS, G * N),
        gdt.T.reshape(1, ROWS, H),
        grad_a.reshape(H),
        grad_k.reshape(H),
        grad_t.reshape(H),
    )


def solution(mesh):
    rows = P("dp", "ctx", None)
    return jax.shard_map(
        shards,
        mesh=mesh,
        in_specs=(rows, rows, rows, rows, P("dp", "ctx"), P(), P(), P(), rows),
        out_specs=(rows, rows, rows, rows, rows, P(), P(), P()),
        check_vma=False,
    )
```
